32 devices in a mesh: section: 2 (over x), dp: 8 (over z, core), tensor: 2 (over y).
Axes of the slice: x: 2, y: 2, z: 4, core: 2. Of those that a mesh axis runs over, the one named last changes fastest.
Arguments:
- ends_in: bfloat16 [2, 2, 2048, 2048], P('section', None, ('dp', 'tensor')), may hold values from -6 to 6
- pieces: int32 [2, 2], replicated, may hold values from 0 to 1792, as said below
- w_query: bfloat16 [2, 2048, 2048], P('section', 'dp', 'tensor'), may hold values from -0.125 to 0.125
- w_keyval: bfloat16 [2, 2048, 256], P('section', ('dp', 'tensor')), may hold values from -0.125 to 0.125
- w_output: bfloat16 [2, 2048, 2048], P('section', 'tensor', 'dp'), may hold values from -1.5 to 1.5
- w_hidden: bfloat16 [2, 2048, 8192], P('section', 'dp', 'tensor'), may hold values from -0.125 to 0.125
- w_project: bfloat16 [2, 8192, 2048], P('section', 'tensor', 'dp'), may hold values from -0.0625 to 0.0625
- norm_params: bfloat16 [2, 4, 2048], P('section', None, ('dp', 'tensor')), as said below
Outputs:
- ends_out: float32 [2, 2, 2048, 2048], P('section', None, ('dp', 'tensor'))
- grad_query: float32 [2, 2048, 2048], P('section', 'dp', 'tensor')
- grad_keyval: float32 [2, 2048, 256], P('section', ('dp', 'tensor'))
- grad_output: float32 [2, 2048, 2048], P('section', 'tensor', 'dp')
- grad_hidden: float32 [2, 2048, 8192], P('section', 'dp', 'tensor')
- grad_project: float32 [2, 8192, 2048], P('section', 'tensor', 'dp')
- grad_norms: float32 [2, 3, 2048], P('section', None, ('dp', 'tensor'))
- grad_shift: float32 [2, 2048], P('section', ('dp', 'tensor'))
The draws below stay inside these ranges and needn't reach their ends.
Inputs may be any that keep to these rules, and one draw needn't show every extreme that they name: Each sequence has 2 picture pieces of 256 positions; the j-th starts between j * (1024) and (j + 1) * 1024 - 256. `norm_params`: gains in rows 0 and 2 lie between 0.5 and 1.5.
All inputs are finite; a program needn't handle non-finite values.
Results may differ from the reference program's by a relative error of at most 0.02.
Values may be sent and summed in bfloat16 or wider, within the bound.
No kernel may reach another device: no remote copies, remote signals or barrier semaphores. Data moves between devices by JAX's collectives and lax.ppermute only.
A program may use at most 384 MiB of HBM per device.

```python
import jax
import jax.numpy as jnp
from jax import lax

D = 2048
HEADS = 16
HEAD = 128
FF = 8192
SPAN = 256
PIECES = 2
LEN = 2048
SEQS = 2


def draw_pieces(key, part):
    region = LEN // PIECES
    offsets = jax.random.randint(key, (SEQS, PIECES), 0, region - SPAN + 1)
    starts = offsets + jnp.arange(PIECES, dtype=jnp.int32)[None, :] * region
    starts = starts.at[0, 0].set(0)
    starts = starts.at[SEQS - 1, PIECES - 1].set(LEN - SPAN)
    return starts.astype(jnp.int32)


def draw_norm_params(key, part):
    first_key, second_key = jax.random.split(jax.random.fold_in(key, 7))
    gains = jax.random.uniform(first_key, (2, 2, D), jnp.float32, 0.5, 1.5)
    biases = 0.5 * jax.random.normal(second_key, (2, 2, D), jnp.float32)
    table = jnp.stack([gains[:, 0], biases[:, 0], gains[:, 1], biases[:, 1]], axis=1)
    return table.astype(jnp.bfloat16)


def shard_levels(own_key, dims, cuts, smallest, high):
    factor_of, own = 1.0, jax.random.fold_in(own_key, 6)
    for axis_at, shards_of in cuts:
        heights = jnp.exp(jax.random.uniform(jax.random.fold_in(own, axis_at), (shards_of,), jnp.float32, smallest / len(cuts), high / len(cuts)))
        factor_of = factor_of * jnp.repeat(heights, dims[axis_at] // shards_of).reshape([-1 if axis == axis_at else 1 for axis in range(len(dims))])
    return factor_of


def scatter_about(key, shape, scale, reach, cuts=(), kind=jnp.bfloat16):
    factor_of = shard_levels(key, shape, cuts, -0.22, 0.18) if cuts else 1.0
    array = jax.random.normal(key, shape, jnp.float32) * scale * factor_of
    return jnp.minimum(jnp.maximum(array, -reach), reach).astype(kind)


def setup_inputs(seed: int = 0) -> dict:
    key_of = jax.random.split(jax.random.key(seed), 9)
    ends_in = scatter_about(key_of[0], (2, SEQS, LEN, D), 1.0, 6.0, ((0, 2), (2, 16)))
    pieces = draw_pieces(jax.random.fold_in(key_of[8], 71), 0)
    w_query = scatter_about(key_of[2], (2, D, HEADS * HEAD), D ** -0.5, 0.125, ((0, 2), (1, 8), (2, 2)))
    w_keyval = scatter_about(key_of[3], (2, D, 2 * HEAD), D ** -0.5, 0.125, ((0, 2), (1, 16)))
    w_output = scatter_about(key_of[4], (2, HEADS * HEAD, D), 16 ** -0.5, 1.5, ((0, 2), (1, 2), (2, 8)))
    w_hidden = scatter_about(key_of[5], (2, D, FF), D ** -0.5, 0.125, ((0, 2), (1, 8), (2, 2)))
    w_project = scatter_about(key_of[6], (2, FF, D), FF ** -0.5, 0.0625, ((0, 2), (1, 2), (2, 8)))
    norm_params = draw_norm_params(jax.random.fold_in(key_of[8], 71), 0)
    return {"ends_in": ends_in, "pieces": pieces, "w_query": w_query, "w_keyval": w_keyval, "w_output": w_output, "w_hidden": w_hidden, "w_project": w_project, "norm_params": norm_params}


@jax.custom_vjp
def low(v):
    return lax.optimization_barrier(v.astype(jnp.bfloat16)).astype(jnp.float32)

@jax.custom_vjp
def low_back(v):
    return v

def low_keep(v):
    return (low(v), None)

def low_pass(kept, grad):
    return (grad,)

def back_keep(v):
    return (v, None)

def back_low(kept, grad):
    return (low(grad),)
low.defvjp(low_keep, low_pass)
low_back.defvjp(back_keep, back_low)
EPSILON = 1e-05
NEGATIVE = -1000000000.0

def layer_norm(values, scale_row, shift_row):
    centered = values - lax.optimization_barrier(jnp.mean(values, -1, keepdims=True))
    spread = lax.optimization_barrier(jnp.mean(centered * centered, -1, keepdims=True))
    return centered * lax.rsqrt(spread + EPSILON) * scale_row + shift_row

def matmul(left, right):
    return jnp.einsum('...d,de->...e', left, right, precision=lax.Precision.HIGHEST)

def attend_one(operands):
    queries, keyval, starts = operands
    position = jnp.arange(LEN, dtype=jnp.int32)
    inside = (position[None, :] >= starts[:, None]) & (position[None, :] < starts[:, None] + SPAN)
    shared_piece = jnp.any(inside[:, :, None] & inside[:, None, :], axis=0)
    allowed = (position[None, :] <= position[:, None]) | shared_piece
    queries_three = queries.reshape(LEN, HEADS, HEAD)
    keys_part = keyval[:, :HEAD]
    values_part = keyval[:, HEAD:]
    raw_scores = low_back(jnp.einsum('qhd,kd->hqk', queries_three, keys_part, precision=lax.Precision.HIGHEST))
    scores = jnp.where(allowed[None], raw_scores * HEAD ** (-0.5), NEGATIVE)
    peak = lax.optimization_barrier(jnp.max(scores, -1, keepdims=True))
    expo = jnp.exp(scores - peak)
    probs = expo / lax.optimization_barrier(jnp.sum(expo, -1, keepdims=True))
    attended = jnp.einsum('hqk,kd->qhd', low(probs), values_part, precision=lax.Precision.HIGHEST)
    return low_back(low(attended)).reshape(LEN, HEADS * HEAD)

def layer(inputs, query_mat, keyval_mat, output_mat, hidden_mat, project_mat, norm_table, pieces):
    normed = low(layer_norm(inputs, norm_table[0], norm_table[1]))
    queries = low_back(low(matmul(normed, query_mat)))
    keyval = low_back(low(matmul(normed, keyval_mat)))
    attended = lax.map(jax.checkpoint(attend_one), (queries, keyval, pieces))
    middle = inputs + low_back(matmul(attended, output_mat))
    mixed = low(layer_norm(middle, norm_table[2], norm_table[3]))
    hidden_pre = low_back(matmul(mixed, hidden_mat))
    hidden_act = low(jax.nn.gelu(hidden_pre, approximate=True))
    return middle + low_back(matmul(hidden_act, project_mat))

def forward(first_in, query_all, keyval_all, output_all, hidden_all, project_all, norm_all, pieces):
    between = layer(first_in, query_all[0], keyval_all[0], output_all[0], hidden_all[0], project_all[0], norm_all[0], pieces)
    between = low_back(low(between))
    return layer(between, query_all[1], keyval_all[1], output_all[1], hidden_all[1], project_all[1], norm_all[1], pieces)

def reference(ends_in, pieces, w_query, w_keyval, w_output, w_hidden, w_project, norm_params):
    first_in = ends_in[0].astype(jnp.float32)
    cotangent = ends_in[1].astype(jnp.float32)
    params = (w_query.astype(jnp.float32), w_keyval.astype(jnp.float32), w_output.astype(jnp.float32), w_hidden.astype(jnp.float32), w_project.astype(jnp.float32), norm_params.astype(jnp.float32))

    def whole(first_value, query_all, keyval_all, output_all, hidden_all, project_all, norm_all):
        return forward(first_value, query_all, keyval_all, output_all, hidden_all, project_all, norm_all, pieces)
    result, pull_back = jax.vjp(whole, first_in, *params)
    grads = pull_back(cotangent)
    ends_out = jnp.stack([grads[0], result])
    norm_grads = grads[6]
    return (ends_out, grads[1], grads[2], grads[3], grads[4], grads[5], norm_grads[:, :3], norm_grads[:, 3])
```

```python
import jax
import jax.numpy as jnp
from jax import lax
from jax.sharding import PartitionSpec as P

SPAN = 256
EPSILON = 1e-05
NEGATIVE = -1000000000.0
BF16 = jnp.bfloat16
F32 = jnp.float32


def dot(left, right, dims):
    return lax.dot_general(left, right, ((dims[0], dims[1]), ((), ())), preferred_element_type=F32)


def swap_quad(block, offset):
    size = lax.axis_size("section") * lax.axis_size("tensor")
    return lax.ppermute(block, ("section", "tensor"), [(i, i ^ offset) for i in range(size)])


def swap_dp(block, offset):
    return lax.ppermute(block, "dp", [(i, i ^ offset) for i in range(lax.axis_size("dp"))])


def quad_size():
    return lax.axis_size("section") * lax.axis_size("tensor")


def spread(block):
    return jnp.concatenate([block] + [swap_quad(block, k) for k in range(1, quad_size())], 0)


def collect(partial):
    rows = partial.shape[0] // quad_size()
    total = partial[:rows].astype(F32)
    for k in range(1, quad_size()):
        total = total + swap_quad(partial[k * rows : (k + 1) * rows], k).astype(F32)
    return total


def gather_dp(block):
    count = lax.axis_size("dp")
    far = [block] + [swap_dp(block, 2 * j) for j in range(1, count // 2)]
    near = swap_dp(jnp.stack(far), 1)
    return jnp.stack(far), near


def scatter_dp(near_even, near_odd):
    halves = near_even + swap_dp(near_odd.astype(BF16), 1).astype(F32)
    total = halves[0]
    for j in range(1, halves.shape[0]):
        total = total + swap_dp(halves[j].astype(BF16), 2 * j).astype(F32)
    return total


def scatter_all(blocks, wire):
    sections, count, tensors = blocks.shape[:3]
    me_s, me_d, me_t = lax.axis_index("section"), lax.axis_index("dp"), lax.axis_index("tensor")

    def pick(s, t):
        one = lax.dynamic_index_in_dim(blocks, me_s ^ s, 0, keepdims=False)
        return lax.dynamic_index_in_dim(one, me_t ^ t, 1, keepdims=False)

    total = pick(0, 0)
    for k in range(1, sections * tensors):
        total = total + swap_quad(pick(k // tensors, k % tensors).astype(wire), k).astype(F32)
    pairs = total.reshape((count // 2, 2) + total.shape[1:])
    core = me_d % 2
    kept = lax.dynamic_index_in_dim(pairs, core, 1, keepdims=False)
    given = lax.dynamic_index_in_dim(pairs, 1 - core, 1, keepdims=False)
    kept = kept + swap_dp(given.astype(wire), 1).astype(F32)
    place = me_d // 2
    result = lax.dynamic_index_in_dim(kept, place, 0, keepdims=False)
    for j in range(1, count // 2):
        piece = lax.dynamic_index_in_dim(kept, place ^ j, 0, keepdims=False)
        result = result + swap_dp(piece.astype(wire), 2 * j).astype(F32)
    return result


def gather_all(block):
    sections, count, tensors = (lax.axis_size(a) for a in ("section", "dp", "tensor"))
    me_s, me_d, me_t = lax.axis_index("section"), lax.axis_index("dp"), lax.axis_index("tensor")
    even, odd = gather_dp(block)
    mine = jnp.stack([even, odd], 1).reshape((count,) + block.shape)
    parts = [mine] + [swap_quad(mine, k) for k in range(1, sections * tensors)]
    whole = jnp.zeros((sections, count, tensors) + block.shape, block.dtype)
    for k, part in enumerate(parts):
        for j in range(count):
            index = (me_s ^ (k // tensors), me_d ^ j, me_t ^ (k % tensors)) + (0,) * block.ndim
            whole = lax.dynamic_update_slice(whole, part[j][None, None, None], index)
    return whole


def layer_norm(values, scale_row, shift_row):
    centered = values - jnp.mean(values, -1, keepdims=True)
    spread_of = jnp.mean(centered * centered, -1, keepdims=True)
    return centered * lax.rsqrt(spread_of + EPSILON) * scale_row + shift_row


def gelu_tanh(values):
    return jax.nn.gelu(values, approximate=True)


def allowed_keys(starts, query_pos, key_pos):
    causal = key_pos[None, :] <= query_pos[:, None]
    query_in = (query_pos[None, :] >= starts[:, None]) & (query_pos[None, :] < starts[:, None] + SPAN)
    key_in = (key_pos[None, :] >= starts[:, None]) & (key_pos[None, :] < starts[:, None] + SPAN)
    return causal | jnp.any(query_in[:, :, None] & key_in[:, None, :], axis=0)


def scores_of(queries, keys, allowed):
    head = keys.shape[-1]
    scores = jnp.einsum("sqhd,skd->shqk", queries, keys, preferred_element_type=F32) * head**-0.5
    return jnp.where(allowed[:, None], scores, NEGATIVE)


def attend_forward(queries, keyval, allowed):
    head = keyval.shape[-1] // 2
    four = queries.reshape(allowed.shape[0], allowed.shape[1], -1, head)
    scores = scores_of(four, keyval[..., :head], allowed)
    peak = jnp.max(scores, -1, keepdims=True)
    log_total = peak + jnp.log(jnp.sum(jnp.exp(scores - peak), -1, keepdims=True))
    probs = jnp.exp(scores - log_total).astype(BF16)
    out = jnp.einsum("shqk,skd->sqhd", probs, keyval[..., head:], preferred_element_type=F32)
    return log_total, out.astype(BF16).reshape(queries.shape)


def attend_backward(queries, keyval, log_total, grad_out, allowed):
    head = keyval.shape[-1] // 2
    shape = (allowed.shape[0], allowed.shape[1], -1, head)
    four, grad_four = queries.reshape(shape), grad_out.reshape(shape)
    keys, values = keyval[..., :head], keyval[..., head:]
    probs = jnp.exp(scores_of(four, keys, allowed) - log_total)
    grad_probs = jnp.einsum("sqhd,skd->shqk", grad_four, values, preferred_element_type=F32)
    grad_values = jnp.einsum(
        "shqk,sqhd->skd", probs.astype(BF16), grad_four, preferred_element_type=F32
    )
    weighted = jnp.sum(probs * grad_probs, -1, keepdims=True)
    grad_scores = (probs * (grad_probs - weighted) * head**-0.5).astype(BF16)
    grad_queries = jnp.einsum("shqk,skd->sqhd", grad_scores, keys, preferred_element_type=F32)
    grad_keys = jnp.einsum("shqk,sqhd->skd", grad_scores, four, preferred_element_type=F32)
    return grad_queries.astype(BF16).reshape(queries.shape), jnp.concatenate(
        [grad_keys, grad_values], -1
    )


def gather_keyval(block):
    even, odd = gather_dp(block)
    mine = jnp.concatenate([even, odd], 0)
    parts = [mine] + [swap_quad(mine, k) for k in range(1, quad_size())]
    return jnp.stack(parts).reshape(lax.axis_size("section"), -1, block.shape[-1])


def scatter_keyval(partial, rows):
    count = lax.axis_size("dp")
    blocks = partial.reshape(quad_size(), count * rows, partial.shape[-1])
    total = blocks[0]
    for k in range(1, quad_size()):
        total = total + swap_quad(blocks[k].astype(BF16), k).astype(F32)
    halves = total.reshape(2, count // 2, rows, partial.shape[-1])
    return scatter_dp(halves[0], halves[1])


def layer_forward(inputs, weights, allowed):
    query_mat, keyval_mat, output_mat, hidden_mat, project_mat, norms = weights
    normed = layer_norm(inputs, norms[0], norms[1]).astype(BF16)
    keyval = gather_keyval(dot(normed, keyval_mat, ((1,), (0,))).astype(BF16))
    normed_all = spread(normed)
    queries = dot(normed_all, query_mat, ((1,), (0,))).astype(BF16)
    log_total, attended = attend_forward(queries, keyval, allowed)
    middle = inputs + collect(dot(attended, output_mat, ((1,), (0,))).astype(BF16))
    mixed_all = spread(layer_norm(middle, norms[2], norms[3]).astype(BF16))
    hidden_pre = dot(mixed_all, hidden_mat, ((1,), (0,)))
    hidden_act = gelu_tanh(hidden_pre).astype(BF16)
    outputs = middle + collect(dot(hidden_act, project_mat, ((1,), (0,))).astype(BF16))
    saved = (normed, normed_all, keyval, queries, log_total, attended)
    return outputs, saved + (middle, mixed_all, hidden_pre, hidden_act)


def layer_backward(inputs, grad_out, weights, allowed, saved):
    query_mat, keyval_mat, output_mat, hidden_mat, project_mat, norms = weights
    normed, normed_all, keyval, queries, log_total, attended = saved[:6]
    middle, mixed_all, hidden_pre, hidden_act = saved[6:]
    rows = inputs.shape[0]
    grad_branch = spread(grad_out.astype(BF16))
    grad_project = dot(hidden_act, grad_branch, ((0,), (0,))).astype(BF16)
    grad_act = dot(grad_branch, project_mat, ((1,), (1,)))
    grad_pre = jax.vjp(gelu_tanh, hidden_pre)[1](grad_act)[0].astype(BF16)
    grad_hidden = dot(mixed_all, grad_pre, ((0,), (0,))).astype(BF16)
    grad_mixed = collect(dot(grad_pre, hidden_mat, ((1,), (1,))).astype(BF16))
    pull = jax.vjp(layer_norm, middle, norms[2], norms[3])[1]
    grad_mid, grad_gain_two, grad_bias_two = pull(grad_mixed)
    grad_middle = grad_out + grad_mid
    grad_rows = spread(grad_middle.astype(BF16))
    grad_output = dot(attended, grad_rows, ((0,), (0,))).astype(BF16)
    grad_attended = dot(grad_rows, output_mat, ((1,), (1,))).astype(BF16)
    grad_queries, grad_kv = attend_backward(queries, keyval, log_total, grad_attended, allowed)
    grad_query = dot(normed_all, grad_queries, ((0,), (0,))).astype(BF16)
    grad_keyval = scatter_keyval(grad_kv, rows).astype(BF16)
    grad_keyval_mat = dot(normed, grad_keyval, ((0,), (0,)))
    grad_normed = collect(dot(grad_queries, query_mat, ((1,), (1,))).astype(BF16))
    grad_normed = grad_normed + dot(grad_keyval, keyval_mat, ((1,), (1,)))
    pull = jax.vjp(layer_norm, inputs, norms[0], norms[1])[1]
    grad_in, grad_gain_one, grad_bias_one = pull(grad_normed)
    table = jnp.stack([grad_gain_one, grad_bias_one, grad_gain_two, grad_bias_two])
    grads = (grad_query, grad_output, grad_hidden, grad_project)
    return grad_middle + grad_in, grads, grad_keyval_mat, table


CUT = (1, 0, 1, 0)


def local(ends_in, pieces, w_query, w_keyval, w_output, w_hidden, w_project, norm_params):
    section = lax.axis_index("section")
    tensor = lax.axis_index("tensor")
    place = lax.axis_index("dp")
    first = section == 0
    count, tensors = lax.axis_size("dp"), lax.axis_size("tensor")
    rows, width = ends_in.shape[2:]

    given = lax.dynamic_index_in_dim(ends_in[0], 1 - section, 0, keepdims=False)
    kept = lax.dynamic_index_in_dim(ends_in[0], section, 0, keepdims=False)
    taken = lax.ppermute(given, "section", [(0, 1), (1, 0)])
    inputs = jnp.where(first, kept, taken).astype(F32)
    cotangent = jnp.where(first, taken, kept).astype(F32)

    depth = w_keyval.shape[1]
    columns = w_keyval.shape[2]
    table = jnp.pad(norm_params[0].reshape(-1), (0, 16 * columns - 4 * depth))
    small = gather_all(jnp.concatenate([w_keyval[0], table.reshape(16, columns)], 0))
    keyval_mats = small[..., :depth, :].reshape(2, width, columns)
    norms = small[..., depth:, :].reshape(2, count * tensors, 16 * columns)
    norms = norms[..., : 4 * depth].reshape(2, count * tensors, 4, depth)
    norms = jnp.swapaxes(norms, 1, 2).reshape(2, 4, width).astype(F32)

    large = (w_query[0], w_output[0], w_hidden[0], w_project[0])

    def quarter(array, cut, index):
        size = array.shape[cut] // 2
        return lax.dynamic_slice_in_dim(array, index * size, size, cut)

    mats = []
    for layer in range(2):
        mine = []
        for array, cut in zip(large, CUT):
            moved = lax.ppermute(
                quarter(array, cut, 1 - section), "section", [(layer, 1 - layer)]
            )
            shard = jnp.where(section == layer, quarter(array, cut, section), moved)
            mine.append(lax.all_gather(shard, "dp", axis=1 - cut, tiled=True))
        mats.append((mine[0], keyval_mats[layer], mine[1], mine[2], mine[3], norms[layer]))

    row = jnp.arange(rows, dtype=jnp.int32)
    turn = tensor ^ jnp.arange(tensors, dtype=jnp.int32)
    query_pos = ((place * tensors + turn)[:, None] * rows + row).reshape(-1)
    order = jnp.concatenate([jnp.arange(0, count, 2), jnp.arange(1, count, 2)]).astype(jnp.int32)
    where = (place ^ order)[None, :] * tensors + turn[:, None]
    key_pos = (where[:, :, None] * rows + row).reshape(-1)
    allowed = jnp.stack(
        [
            allowed_keys(
                lax.dynamic_index_in_dim(pieces, section ^ k, 0, keepdims=False),
                query_pos,
                key_pos,
            )
            for k in range(2)
        ]
    )

    between, saved_one = layer_forward(inputs, mats[0], allowed)
    between = between.astype(BF16).astype(F32)
    outputs, saved_two = layer_forward(between, mats[1], allowed)
    grad_between, grads_two, kv_two, table_two = layer_backward(
        between, cotangent, mats[1], allowed, saved_two
    )
    grad_between = grad_between.astype(BF16).astype(F32)
    grad_inputs, grads_one, kv_one, table_one = layer_backward(
        inputs, grad_between, mats[0], allowed, saved_one
    )

    results = []
    for index, cut in enumerate(CUT):
        halves = []
        for layer, grads in ((1, grads_two), (0, grads_one)):
            own = lax.psum_scatter(grads[index], "dp", scatter_dimension=1 - cut, tiled=True)
            moved = lax.ppermute(own, "section", [(1 - layer, layer)])
            pair = (own, moved) if layer == 0 else (moved, own)
            halves.append(jnp.concatenate(pair, cut).astype(F32))
        results.append(jnp.where(first, halves[1], halves[0])[None])

    kv_blocks = jnp.stack([kv_one, kv_two]).reshape(2, count, tensors, depth, -1)
    kv_result = scatter_all(kv_blocks, BF16)
    tables = jnp.stack([table_one, table_two]).reshape(2, 4, count, tensors, depth)
    table_result = scatter_all(jnp.moveaxis(tables, 1, 3), F32)

    given = jnp.where(first, outputs, grad_inputs).astype(BF16)
    kept = jnp.where(first, grad_inputs, outputs)
    taken = lax.ppermute(given, "section", [(0, 1), (1, 0)]).astype(F32)
    ends_out = jnp.where(first, jnp.stack([kept, taken]), jnp.stack([taken, kept]))
    return (
        ends_out[None],
        results[0],
        kv_result[None],
        results[1],
        results[2],
        results[3],
        table_result[None, :3],
        table_result[None, 3],
    )


def solution(mesh):
    placed = (
        P("section", None, ("dp", "tensor"), None),
        P(),
        P("section", "dp", "tensor"),
        P("section", ("dp", "tensor"), None),
        P("section", "tensor", "dp"),
        P("section", "dp", "tensor"),
        P("section", "tensor", "dp"),
        P("section", None, ("dp", "tensor")),
    )
    return jax.shard_map(
        local,
        mesh=mesh,
        in_specs=placed,
        out_specs=(
            P("section", None, ("dp", "tensor"), None),
            P("section", "dp", "tensor"),
            P("section", ("dp", "tensor"), None),
            P("section", "tensor", "dp"),
            P("section", "dp", "tensor"),
            P("section", "tensor", "dp"),
            P("section", None, ("dp", "tensor")),
            P("section", ("dp", "tensor")),
        ),
        check_vma=False,
    )
```

```python
import functools
import math

import jax
import jax.numpy as jnp
from jax import lax
from jax.experimental import pallas as pl
from jax.experimental.pallas import tpu as pltpu
from jax.sharding import PartitionSpec as P

SPAN = 256
EPSILON = 1e-05
NEGATIVE = -1000000000.0
BF16 = jnp.bfloat16
F32 = jnp.float32
LOG2E = math.log2(math.e)


def dot(left, right, dims):
    return lax.dot_general(left, right, ((dims[0], dims[1]), ((), ())), preferred_element_type=F32)


def swap_quad(block, offset):
    size = lax.axis_size("section") * lax.axis_size("tensor")
    return lax.ppermute(block, ("section", "tensor"), [(i, i ^ offset) for i in range(size)])


def swap_dp(block, offset):
    return lax.ppermute(block, "dp", [(i, i ^ offset) for i in range(lax.axis_size("dp"))])


def quad_size():
    return lax.axis_size("section") * lax.axis_size("tensor")


def spread(block):
    return jnp.concatenate([block] + [swap_quad(block, k) for k in range(1, quad_size())], 0)


def collect(partial):
    rows = partial.shape[0] // quad_size()
    total = partial[:rows].astype(F32)
    for k in range(1, quad_size()):
        total = total + swap_quad(partial[k * rows : (k + 1) * rows], k).astype(F32)
    return total


def gather_dp(block):
    count = lax.axis_size("dp")
    far = [block] + [swap_dp(block, 2 * j) for j in range(1, count // 2)]
    near = swap_dp(jnp.stack(far), 1)
    return jnp.stack(far), near


def scatter_dp(near_even, near_odd):
    halves = near_even + swap_dp(near_odd.astype(BF16), 1).astype(F32)
    total = halves[0]
    for j in range(1, halves.shape[0]):
        total = total + swap_dp(halves[j].astype(BF16), 2 * j).astype(F32)
    return total


def scatter_all(blocks, wire):
    sections, count, tensors = blocks.shape[:3]
    me_s, me_d, me_t = lax.axis_index("section"), lax.axis_index("dp"), lax.axis_index("tensor")

    def pick(s, t):
        one = lax.dynamic_index_in_dim(blocks, me_s ^ s, 0, keepdims=False)
        return lax.dynamic_index_in_dim(one, me_t ^ t, 1, keepdims=False)

    total = pick(0, 0)
    for k in range(1, sections * tensors):
        total = total + swap_quad(pick(k // tensors, k % tensors).astype(wire), k).astype(F32)
    pairs = total.reshape((count // 2, 2) + total.shape[1:])
    core = me_d % 2
    kept = lax.dynamic_index_in_dim(pairs, core, 1, keepdims=False)
    given = lax.dynamic_index_in_dim(pairs, 1 - core, 1, keepdims=False)
    kept = kept + swap_dp(given.astype(wire), 1).astype(F32)
    place = me_d // 2
    result = lax.dynamic_index_in_dim(kept, place, 0, keepdims=False)
    for j in range(1, count // 2):
        piece = lax.dynamic_index_in_dim(kept, place ^ j, 0, keepdims=False)
        result = result + swap_dp(piece.astype(wire), 2 * j).astype(F32)
    return result


def gather_all(block):
    count, tensors = lax.axis_size("dp"), lax.axis_size("tensor")
    me_s, me_d, me_t = lax.axis_index("section"), lax.axis_index("dp"), lax.axis_index("tensor")
    even, odd = gather_dp(block)
    mine = jnp.stack([even, odd], 1).reshape((count,) + block.shape)
    passed = even
    beside = swap_quad(mine, 1)
    across = swap_quad(mine, tensors)
    corner = swap_quad(across, 1)

    def ordered(bit, own, other):
        return jnp.where(bit == 0, jnp.stack([own, other]), jnp.stack([other, own]))

    parts = ordered(me_s, ordered(me_t, mine, beside), ordered(me_t, across, corner))
    whole = jnp.zeros_like(parts)
    for j in range(count):
        whole = lax.dynamic_update_slice_in_dim(whole, parts[:, :, j : j + 1], me_d ^ j, 2)
    return jnp.swapaxes(whole, 1, 2), passed


def layer_norm(values, scale_row, shift_row):
    centered = values - jnp.mean(values, -1, keepdims=True)
    spread_of = jnp.mean(centered * centered, -1, keepdims=True)
    return centered * lax.rsqrt(spread_of + EPSILON) * scale_row + shift_row


def gelu_tanh(values):
    return jax.nn.gelu(values, approximate=True)


def dot_nn(left, right):
    return dot(left, right, ((1,), (0,)))


def dot_nt(left, right):
    return dot(left, right, ((1,), (1,)))


def dot_tn(left, right):
    return dot(left, right, ((0,), (0,)))


def attend_kernel(rows, heads, head, base_ref, limit_ref, query_ref, keyval_ref, out_ref, log_ref, score_ref, prob_ref):
    keys=keyval_ref.shape[1]; queries=query_ref.shape[0]
    blocks=keys//rows
    scale=head**-0.5*LOG2E
    limit=limit_ref[0]
    offset=lax.broadcasted_iota(jnp.int32,(rows,queries),0)
    values_t=keyval_ref[0,:,head:].T
    for h in range(heads):
        query=query_ref[:,h*head:(h+1)*head]
        def scores(b,peak):
            at=pl.ds(pl.multiple_of(b*rows,rows),rows)
            s=dot_nt(keyval_ref[0,at,:head],query)*scale
            s=jnp.where(offset<=limit-base_ref[b],s,NEGATIVE)
            score_ref[h%2,at,:]=s
            return jnp.maximum(peak,jnp.max(s.reshape(rows//8,8,queries),0))
        peak=lax.fori_loop(0,blocks,scores,jnp.full((8,queries),-jnp.inf,F32),unroll=4)
        peak=jnp.max(peak,0,keepdims=True)
        def probs(b,total):
            at=pl.ds(pl.multiple_of(b*rows,rows),rows)
            p=jnp.exp2(score_ref[h%2,at,:]-peak)
            prob_ref[h%2,at,:]=p.astype(BF16)
            return total+jnp.sum(p.reshape(rows//8,8,queries),0)
        total=lax.fori_loop(0,blocks,probs,jnp.zeros((8,queries),F32),unroll=4)
        total=jnp.sum(total,0,keepdims=True)
        out=dot_nn(values_t,prob_ref[h%2])*(1.0/total)
        out_ref[:,h*head:(h+1)*head]=out.T.astype(BF16)
        log_ref[0,h:h+1,:]=peak+jnp.log2(total)

def attend_forward(queries, keyval, limits, bases, rows):
    seqs,keys,two=keyval.shape
    head=two//2; heads=queries.shape[1]//head; count=queries.shape[0]//seqs
    return pl.pallas_call(
        functools.partial(attend_kernel,rows,heads,head),
        grid_spec=pltpu.PrefetchScalarGridSpec(
            num_scalar_prefetch=1, grid=(seqs,),
            in_specs=[pl.BlockSpec((1,1,count),lambda i,*_:(i,0,0)),
                      pl.BlockSpec((count,heads*head),lambda i,*_:(i,0)),
                      pl.BlockSpec((1,keys,two),lambda i,*_:(i,0,0))],
            out_specs=[pl.BlockSpec((count,heads*head),lambda i,*_:(i,0)),
                       pl.BlockSpec((1,heads,count),lambda i,*_:(i,0,0))],
            scratch_shapes=[pltpu.VMEM((2,keys,count),F32),pltpu.VMEM((2,keys,count),BF16)]),
        out_shape=[jax.ShapeDtypeStruct(queries.shape,BF16),jax.ShapeDtypeStruct((seqs,heads,count),F32)],
        compiler_params=pltpu.CompilerParams(vmem_limit_bytes=40*2**20),
        cost_estimate=pl.CostEstimate(flops=4*queries.shape[0]*heads*head*keys,bytes_accessed=4*queries.size+2*keyval.size,transcendentals=queries.shape[0]*heads*keys),
    )(bases,limits,queries,keyval)

def attend_grad_kernel(
    rows, heads, head, base_ref, limit_ref, query_ref, grad_ref, log_ref, keyval_ref,
    dq_ref, dkv_ref, prob_ref, score_ref, exact_ref, slope_ref,
):
    keys = keyval_ref.shape[1]
    queries = query_ref.shape[0]
    blocks = keys // rows
    scale = head**-0.5
    limit = limit_ref[0]
    offset = lax.broadcasted_iota(jnp.int32, (rows, queries), 0)
    keys_t = keyval_ref[0, :, :head].T
    for h in range(heads):
        cols = slice(h * head, (h + 1) * head)
        lanes = slice(h * queries, (h + 1) * queries)
        query = query_ref[:, cols]
        grad = grad_ref[:, cols]
        log = log_ref[0, h : h + 1, :]

        def first(b, weighted):
            at = pl.ds(pl.multiple_of(b * rows, rows), rows)
            s = dot_nt(keyval_ref[0, at, :head], query) * (scale * LOG2E) - log
            s = jnp.where(offset <= limit - base_ref[b], s, NEGATIVE)
            p = jnp.exp2(s)
            dp = dot_nt(keyval_ref[0, at, head:], grad)
            prob_ref[at, lanes] = p.astype(BF16)
            exact_ref[h % 2, at, :] = p
            slope_ref[h % 2, at, :] = dp
            return weighted + jnp.sum((p * dp).reshape(rows // 8, 8, queries), 0)

        weighted = jnp.zeros((8, queries), F32)
        weighted = lax.fori_loop(0, blocks, first, weighted, unroll=4)
        weighted = jnp.sum(weighted, 0, keepdims=True)

        def second(b, carry):
            at = pl.ds(pl.multiple_of(b * rows, rows), rows)
            term = exact_ref[h % 2, at, :] * ((slope_ref[h % 2, at, :] - weighted) * scale)
            score_ref[at, lanes] = term.astype(BF16)
            return carry

        lax.fori_loop(0, blocks, second, 0, unroll=4)
        dq_ref[:, cols] = dot_nn(keys_t, score_ref[:, lanes]).T.astype(BF16)
    stacked_q = jnp.concatenate(
        [query_ref[:, h * head : (h + 1) * head] for h in range(heads)], 0
    )
    stacked_g = jnp.concatenate([grad_ref[:, h * head : (h + 1) * head] for h in range(heads)], 0)
    dkv_ref[0, :, :head] = dot_nn(score_ref[...], stacked_q).astype(BF16)
    dkv_ref[0, :, head:] = dot_nn(prob_ref[...], stacked_g).astype(BF16)


def attend_backward(queries, grad, logs, keyval, limits, bases, rows):
    seqs,keys,two=keyval.shape
    head=two//2; heads=queries.shape[1]//head; count=queries.shape[0]//seqs
    q_spec=pl.BlockSpec((count,heads*head),lambda i,*_:(i,0))
    return pl.pallas_call(
        functools.partial(attend_grad_kernel,rows,heads,head),
        grid_spec=pltpu.PrefetchScalarGridSpec(
            num_scalar_prefetch=1, grid=(seqs,),
            in_specs=[pl.BlockSpec((1,1,count),lambda i,*_:(i,0,0)),q_spec,q_spec,
                      pl.BlockSpec((1,heads,count),lambda i,*_:(i,0,0)),
                      pl.BlockSpec((1,keys,two),lambda i,*_:(i,0,0))],
            out_specs=[q_spec,pl.BlockSpec((1,keys,two),lambda i,*_:(i,0,0))],
            scratch_shapes=[pltpu.VMEM((keys,heads*count),BF16),pltpu.VMEM((keys,heads*count),BF16),pltpu.VMEM((2,keys,count),F32),pltpu.VMEM((2,keys,count),F32)]),
        out_shape=[jax.ShapeDtypeStruct(queries.shape,BF16),jax.ShapeDtypeStruct(keyval.shape,BF16)],
        compiler_params=pltpu.CompilerParams(vmem_limit_bytes=40*2**20),
        cost_estimate=pl.CostEstimate(flops=10*queries.shape[0]*heads*head*keys,bytes_accessed=8*queries.size+4*keyval.size,transcendentals=queries.shape[0]*heads*keys),
    )(bases,limits,queries,grad,logs,keyval)


def gather_keyval(block):
    even, odd = gather_dp(block)
    mine = jnp.concatenate([even, odd], 0)
    parts = [mine] + [swap_quad(mine, k) for k in range(1, quad_size())]
    return jnp.stack(parts).reshape(lax.axis_size("section"), -1, block.shape[-1]), even


def scatter_keyval(partial, rows):
    count = lax.axis_size("dp")
    blocks = partial.reshape(quad_size(), count * rows, partial.shape[-1])
    total = blocks[0]
    for k in range(1, quad_size()):
        total = total + swap_quad(blocks[k].astype(BF16), k).astype(F32)
    halves = total.reshape(2, count // 2, rows, partial.shape[-1])
    return scatter_dp(halves[0], halves[1])


def send_chips(block, pairs):
    return lax.ppermute(block, "dp", [(2 * a + c, 2 * b + c) for a, b in pairs for c in (0, 1)])


def gather_chips(block):
    chips = lax.axis_size("dp") // 2
    if chips != 4:
        return [block] + [swap_dp(block, 2 * j) for j in range(1, chips)]
    two = send_chips(block, [(0, 2), (2, 0), (1, 3), (3, 1)])
    one = send_chips(block, [(0, 1), (1, 0), (2, 3), (3, 2)])
    three = send_chips(block, [(1, 2), (2, 1)])
    return [block, one, two, three + send_chips(two, [(2, 3), (1, 0)])]


def gather_cores(far):
    count = lax.axis_size("dp")
    place = lax.axis_index("dp")
    near = swap_dp(jnp.stack(far), 1)
    whole = jnp.zeros((count,) + far[0].shape, far[0].dtype)
    for j in range(count // 2):
        whole = lax.dynamic_update_slice_in_dim(whole, far[j][None], place ^ (2 * j), 0)
        whole = lax.dynamic_update_slice_in_dim(whole, near[j][None], place ^ (2 * j + 1), 0)
    return whole.reshape((-1,) + far[0].shape[1:])


def scatter_mat(partial):
    chips = lax.axis_size("dp") // 2
    place = lax.axis_index("dp")
    core, chip = place % 2, place // 2
    pairs = partial.reshape(chips, 2, -1, partial.shape[1])
    kept = lax.dynamic_index_in_dim(pairs, core, 1, keepdims=False).astype(F32)
    given = lax.dynamic_index_in_dim(pairs, 1 - core, 1, keepdims=False)
    kept = (kept + swap_dp(given, 1).astype(F32)).astype(BF16)

    def piece(j):
        return lax.dynamic_index_in_dim(kept, chip ^ j, 0, keepdims=False)

    total = piece(0).astype(F32)
    if chips != 4:
        for j in range(1, chips):
            total = total + swap_dp(piece(j), 2 * j).astype(F32)
        return total
    passed = send_chips(piece(3), [(0, 1), (3, 2)])
    one = send_chips(piece(1), [(0, 1), (1, 0), (2, 3), (3, 2)])
    three = send_chips(piece(3), [(1, 2), (2, 1)])
    two = (piece(2).astype(F32) + passed.astype(F32)).astype(BF16)
    two = send_chips(two, [(0, 2), (2, 0), (1, 3), (3, 1)])
    return total + one.astype(F32) + two.astype(F32) + three.astype(F32)


def after(value, *done):
    held = lax.optimization_barrier((value,) + done)
    return held[0], held[1:]


def attend_part(inputs, pair, keyval_mat, norms, limits, bases):
    rows = inputs.shape[0]
    normed = layer_norm(inputs, norms[0], norms[1]).astype(BF16)
    keyval, passed = gather_keyval(dot_nn(normed, keyval_mat).astype(BF16))
    normed_all = spread(normed)
    queries = dot_nn(normed_all, pair[0]).astype(BF16)
    attended, logs = attend_forward(queries, keyval, limits, bases, rows)
    middle = inputs + collect(dot_nt(attended, pair[1]).astype(BF16))
    return middle, (normed_all, keyval, queries, logs, attended), passed


def mix_part(middle, norms):
    return spread(layer_norm(middle, norms[2], norms[3]).astype(BF16))


def hidden_part(mixed_all, hidden_mat):
    hidden_pre = dot_nn(mixed_all, hidden_mat)
    return hidden_pre, gelu_tanh(hidden_pre).astype(BF16)


def scatter_rows(partial):
    return lax.psum_scatter(partial, "dp", scatter_dimension=0, tiled=True)


def scatter_columns(partial):
    return lax.psum_scatter(partial, "dp", scatter_dimension=1, tiled=True)


def layer_backward(inputs, grad_out, weights, limits, bases, saved, early, late):
    pair, keyval_mat, hidden_mat, project_mat, norms = weights
    normed_all, keyval, queries, logs, attended, middle, mixed_all, hidden_pre, hidden_act = saved
    rows = inputs.shape[0]
    grad_branch = spread(grad_out.astype(BF16))
    grad_act = dot_nt(grad_branch, project_mat)
    grad_pre = jax.vjp(gelu_tanh, hidden_pre)[1](grad_act)[0].astype(BF16)
    hidden_act, _ = after(hidden_act, *early)
    mixed_all, _ = after(mixed_all, *early)
    grad_project = dot_tn(hidden_act, grad_branch).astype(BF16)
    sum_project = scatter_columns(grad_project)
    grad_hidden = dot_tn(mixed_all, grad_pre).astype(BF16)
    sum_hidden = scatter_rows(grad_hidden)
    grad_mixed = collect(dot_nt(grad_pre, hidden_mat).astype(BF16))
    if not early:
        grad_mixed, _ = after(grad_mixed, grad_project, grad_hidden)
    pull = jax.vjp(layer_norm, middle, norms[2], norms[3])[1]
    grad_mid, grad_gain_two, grad_bias_two = pull(grad_mixed)
    grad_middle = grad_out + grad_mid
    grad_rows = spread(grad_middle.astype(BF16))
    grad_attended = dot_nt(grad_rows, pair[1].T).astype(BF16)
    grad_output = dot_tn(grad_rows, attended).astype(BF16)
    held = (grad_output, grad_project, grad_hidden) + late if early else (grad_output,)
    grad_attended, (grad_output, *_) = after(grad_attended, *held)
    grad_queries, grad_kv = attend_backward(
        queries, grad_attended, logs, keyval, limits, bases, rows
    )
    grad_normed = collect(dot_nt(grad_queries, pair[0]).astype(BF16))
    grad_query = dot_tn(normed_all, grad_queries).astype(BF16)
    grad_normed, (grad_query,) = after(grad_normed, grad_query)
    grad_pair = jnp.concatenate([grad_query, grad_output], 1)
    grad_keyval = scatter_keyval(grad_kv, rows).astype(BF16)
    grad_normed = grad_normed + dot_nt(grad_keyval, keyval_mat)
    pull = jax.vjp(layer_norm, inputs, norms[0], norms[1])[1]
    grad_in, grad_gain_one, grad_bias_one = pull(grad_normed)
    table = jnp.stack([grad_gain_one, grad_bias_one, grad_gain_two, grad_bias_two])

    grad_small = dot_tn(normed_all, spread(grad_keyval)).astype(BF16)
    count, tensors = lax.axis_size("dp"), lax.axis_size("tensor")
    grad_small = grad_small.reshape(count, tensors, 2, -1, grad_small.shape[1])
    grad_small = lax.dynamic_index_in_dim(grad_small, lax.axis_index("tensor"), 1, keepdims=False)
    grad_small = lax.dynamic_index_in_dim(grad_small, lax.axis_index("section"), 1, keepdims=False)
    sum_small = scatter_mat(grad_small.reshape(-1, grad_small.shape[-1]))
    return grad_middle + grad_in, (sum_small, sum_hidden, sum_project), grad_pair, table


def local(ends_in, pieces, w_query, w_keyval, w_output, w_hidden, w_project, norm_params):
    section = lax.axis_index("section")
    tensor = lax.axis_index("tensor")
    place = lax.axis_index("dp")
    first = section == 0
    count, tensors = lax.axis_size("dp"), lax.axis_size("tensor")
    rows, width = ends_in.shape[2:]

    given = lax.dynamic_index_in_dim(ends_in[0], 1 - section, 0, keepdims=False)
    kept = lax.dynamic_index_in_dim(ends_in[0], section, 0, keepdims=False)
    taken = lax.ppermute(given, "section", [(0, 1), (1, 0)])
    inputs = jnp.where(first, kept, taken).astype(F32)
    cotangent = jnp.where(first, taken, kept).astype(F32)

    depth = w_keyval.shape[1]
    columns = w_keyval.shape[2]
    table = jnp.pad(norm_params[0].reshape(-1), (0, 16 * columns - 4 * depth))
    small, _ = gather_all(jnp.concatenate([w_keyval[0], table.reshape(16, columns)], 0))
    keyval_mats = small[..., :depth, :].reshape(2, width, columns)
    norms = small[..., depth:, :].reshape(2, count * tensors, 16 * columns)
    norms = norms[..., : 4 * depth].reshape(2, count * tensors, 4, depth)
    norms = jnp.swapaxes(norms, 1, 2).reshape(2, 4, width).astype(F32)

    def quarter(array, cut, index):
        size = array.shape[cut] // 2
        return lax.dynamic_slice_in_dim(array, index * size, size, cut)

    row = jnp.arange(rows, dtype=jnp.int32)
    turn = tensor ^ jnp.arange(tensors, dtype=jnp.int32)
    query_pos = ((place * tensors + turn)[:, None] * rows + row).reshape(-1)
    order = jnp.concatenate([jnp.arange(0, count, 2), jnp.arange(1, count, 2)]).astype(jnp.int32)
    bases = (((place ^ order)[None, :] * tensors + turn[:, None]) * rows).reshape(-1)
    limits = []
    for k in range(2):
        starts = lax.dynamic_index_in_dim(pieces, section ^ k, 0, keepdims=False)[:, None]
        inside = (query_pos >= starts) & (query_pos < starts + SPAN)
        limits.append(jnp.max(jnp.where(inside, starts + SPAN - 1, query_pos), 0))
    limits = jnp.stack(limits)[:, None]

    def both(pick):
        kept = pick(section)
        moved = lax.ppermute(pick(1 - section), "section", [(0, 1), (1, 0)])
        return jnp.where(first, kept, moved), jnp.where(first, moved, kept)

    output_turned = w_output[0].T
    query_both = both(
        lambda k: jnp.concatenate([quarter(w_query[0], 1, k), quarter(output_turned, 1, k)], 1)
    )
    hidden_shard, project_shard = w_hidden[0], w_project[0]
    hidden_both = both(lambda k: quarter(hidden_shard, 1, k))
    project_both = both(lambda k: quarter(project_shard, 0, k))
    def rows_of(array):
        return lax.all_gather(array, "dp", axis=0, tiled=True)

    def columns_of(array):
        return lax.all_gather(array, "dp", axis=1, tiled=True)

    pair_one = jnp.split(rows_of(query_both[0]), 2, axis=1)
    pair_two = jnp.split(rows_of(query_both[1]), 2, axis=1)
    hidden_both, _ = after(hidden_both, norms)

    middle_one, saved_one, passed = attend_part(
        inputs, pair_one, keyval_mats[0], norms[0], limits, bases
    )
    project_both, _ = after(project_both, passed)
    project_one, project_two = (columns_of(p) for p in project_both)
    hidden_two = rows_of(hidden_both[1])
    hidden_one = rows_of(hidden_both[0])
    mixed_one = mix_part(middle_one, norms[0])
    pre_one, act_one = hidden_part(mixed_one, hidden_one)
    between = middle_one + collect(dot_nn(act_one, project_one).astype(BF16))
    between = between.astype(BF16).astype(F32)

    middle_two, saved_two, _ = attend_part(between, pair_two, keyval_mats[1], norms[1], limits, bases)
    mixed_two = mix_part(middle_two, norms[1])
    cotangent, _ = after(cotangent, mixed_two)
    pre_two, act_two = hidden_part(mixed_two, hidden_two)
    outputs = middle_two + collect(dot_nn(act_two, project_two).astype(BF16))

    grad_between, sums_two, grad_pair, table_two = layer_backward(
        between,
        cotangent,
        (pair_two, keyval_mats[1], hidden_two, project_two, norms[1]),
        limits,
        bases,
        saved_two + (middle_two, mixed_two, pre_two, act_two),
        (),
        (),
    )
    grad_between = grad_between.astype(BF16)
    grad_pair, _ = after(grad_pair, grad_between)
    sum_pair_two = scatter_rows(grad_pair)
    grad_between = grad_between.astype(F32)
    grad_inputs, sums_one, grad_pair, table_one = layer_backward(
        inputs,
        grad_between,
        (pair_one, keyval_mats[0], hidden_one, project_one, norms[0]),
        limits,
        bases,
        saved_one + (middle_one, mixed_one, pre_one, act_one),
        sums_two[1:],
        (),
    )
    sum_pair_one = scatter_rows(after(grad_pair, *sums_one[1:])[0])
    halves_two = jnp.split(sum_pair_two, 2, axis=1)
    halves_one = jnp.split(sum_pair_one, 2, axis=1)
    sums_two = (halves_two[0], sums_two[0], halves_two[1]) + sums_two[1:]
    sums_one = (halves_one[0], sums_one[0], halves_one[1]) + sums_one[1:]

    results = []
    for index, cut in enumerate((1, 0, 1, 1, 0)):
        halves = []
        for layer, sums in ((1, sums_two), (0, sums_one)):
            own = sums[index].astype(BF16)
            moved = lax.ppermute(own, "section", [(1 - layer, layer)])
            pair = (own, moved) if layer == 0 else (moved, own)
            halves.append(jnp.concatenate(pair, cut))
        results.append(jnp.where(first, halves[1], halves[0]).astype(F32)[None])

    tables = jnp.stack([table_one, table_two]).reshape(2, 4, count, tensors, depth)
    table_result = scatter_all(jnp.moveaxis(tables, 1, 3), F32)

    given = jnp.where(first, outputs, grad_inputs).astype(BF16)
    kept = jnp.where(first, grad_inputs, outputs)
    taken = lax.ppermute(given, "section", [(0, 1), (1, 0)]).astype(F32)
    ends_out = jnp.where(first, jnp.stack([kept, taken]), jnp.stack([taken, kept]))
    return (
        ends_out[None],
        results[0],
        results[1],
        jnp.swapaxes(results[2], 1, 2),
        results[3],
        results[4],
        table_result[None, :3],
        table_result[None, 3],
    )


def solution(mesh):
    placed = (
        P("section", None, ("dp", "tensor"), None),
        P(),
        P("section", "dp", "tensor"),
        P("section", ("dp", "tensor"), None),
        P("section", "tensor", "dp"),
        P("section", "dp", "tensor"),
        P("section", "tensor", "dp"),
        P("section", None, ("dp", "tensor")),
    )
    return jax.shard_map(
        local,
        mesh=mesh,
        in_specs=placed,
        out_specs=(
            P("section", None, ("dp", "tensor"), None),
            P("section", "dp", "tensor"),
            P("section", ("dp", "tensor"), None),
            P("section", "tensor", "dp"),
            P("section", "dp", "tensor"),
            P("section", "tensor", "dp"),
            P("section", None, ("dp", "tensor")),
            P("section", ("dp", "tensor")),
        ),
        check_vma=False,
    )
```

```python
import functools
import math

import jax
import jax.numpy as jnp
from jax import lax
from jax.experimental import pallas as pl
from jax.experimental.pallas import tpu as pltpu
from jax.sharding import PartitionSpec as P

SPAN = 256
EPSILON = 1e-05
NEGATIVE = -1000000000.0
BF16 = jnp.bfloat16
F32 = jnp.float32
LOG2E = math.log2(math.e)


def dot(left, right, dims):
    return lax.dot_general(left, right, ((dims[0], dims[1]), ((), ())), preferred_element_type=F32)


def swap_quad(block, offset):
    size = lax.axis_size("section") * lax.axis_size("tensor")
    return lax.ppermute(block, ("section", "tensor"), [(i, i ^ offset) for i in range(size)])


def swap_dp(block, offset):
    return lax.ppermute(block, "dp", [(i, i ^ offset) for i in range(lax.axis_size("dp"))])


def quad_size():
    return lax.axis_size("section") * lax.axis_size("tensor")


def spread_blocks(block):
    return [block] + [swap_quad(block, k) for k in range(1, quad_size())]


def spread(block):
    return jnp.concatenate(spread_blocks(block), 0)


def collect_blocks(blocks):
    total = blocks[0].astype(F32)
    for k in range(1, quad_size()):
        total = total + swap_quad(blocks[k].astype(BF16), k).astype(F32)
    return total


def collect(partial):
    return collect_blocks(jnp.split(partial, quad_size(), 0))


def gather_dp(block):
    count = lax.axis_size("dp")
    far = [block] + [swap_dp(block, 2 * j) for j in range(1, count // 2)]
    near = swap_dp(jnp.stack(far), 1)
    return jnp.stack(far), near


def scatter_dp(near_even, near_odd):
    halves = near_even + swap_dp(near_odd.astype(BF16), 1).astype(F32)
    total = halves[0]
    for j in range(1, halves.shape[0]):
        total = total + swap_dp(halves[j].astype(BF16), 2 * j).astype(F32)
    return total


def scatter_all(blocks, wire):
    sections, count, tensors = blocks.shape[:3]
    me_s, me_d, me_t = lax.axis_index("section"), lax.axis_index("dp"), lax.axis_index("tensor")

    def pick(s, t):
        one = lax.dynamic_index_in_dim(blocks, me_s ^ s, 0, keepdims=False)
        return lax.dynamic_index_in_dim(one, me_t ^ t, 1, keepdims=False)

    total = pick(0, 0)
    for k in range(1, sections * tensors):
        total = total + swap_quad(pick(k // tensors, k % tensors).astype(wire), k).astype(F32)
    pairs = total.reshape((count // 2, 2) + total.shape[1:])
    core = me_d % 2
    kept = lax.dynamic_index_in_dim(pairs, core, 1, keepdims=False)
    given = lax.dynamic_index_in_dim(pairs, 1 - core, 1, keepdims=False)
    kept = kept + swap_dp(given.astype(wire), 1).astype(F32)
    place = me_d // 2
    result = lax.dynamic_index_in_dim(kept, place, 0, keepdims=False)
    for j in range(1, count // 2):
        piece = lax.dynamic_index_in_dim(kept, place ^ j, 0, keepdims=False)
        result = result + swap_dp(piece.astype(wire), 2 * j).astype(F32)
    return result


def gather_all(block):
    count, tensors = lax.axis_size("dp"), lax.axis_size("tensor")
    me_s, me_d, me_t = lax.axis_index("section"), lax.axis_index("dp"), lax.axis_index("tensor")
    even, odd = gather_dp(block)
    mine = jnp.stack([even, odd], 1).reshape((count,) + block.shape)
    passed = even
    beside = swap_quad(mine, 1)
    across = swap_quad(mine, tensors)
    corner = swap_quad(across, 1)

    def ordered(bit, own, other):
        return jnp.where(bit == 0, jnp.stack([own, other]), jnp.stack([other, own]))

    parts = ordered(me_s, ordered(me_t, mine, beside), ordered(me_t, across, corner))
    whole = jnp.zeros_like(parts)
    for j in range(count):
        whole = lax.dynamic_update_slice_in_dim(whole, parts[:, :, j : j + 1], me_d ^ j, 2)
    return jnp.swapaxes(whole, 1, 2), passed


def layer_norm(values, scale_row, shift_row):
    centered = values - jnp.mean(values, -1, keepdims=True)
    spread_of = jnp.mean(centered * centered, -1, keepdims=True)
    return centered * lax.rsqrt(spread_of + EPSILON) * scale_row + shift_row


def gelu_tanh(values):
    return jax.nn.gelu(values, approximate=True)


def dot_nn(left, right):
    return dot(left, right, ((1,), (0,)))


def dot_nt(left, right):
    return dot(left, right, ((1,), (1,)))


def dot_tn(left, right):
    return dot(left, right, ((0,), (0,)))


def attend_kernel(rows, heads, head, base_ref, limit_ref, query_ref, keyval_ref, out_ref, log_ref, score_ref, prob_ref):
    keys=keyval_ref.shape[1]; queries=query_ref.shape[0]
    blocks=keys//rows
    scale=head**-0.5*LOG2E
    limit=limit_ref[0]
    offset=lax.broadcasted_iota(jnp.int32,(rows,queries),0)
    values_t=keyval_ref[0,:,head:].T
    for h in range(heads):
        query=query_ref[:,h*head:(h+1)*head]
        def scores(b,peak):
            at=pl.ds(pl.multiple_of(b*rows,rows),rows)
            s=dot_nt(keyval_ref[0,at,:head],query)*scale
            s=jnp.where(offset<=limit-base_ref[b],s,NEGATIVE)
            score_ref[h%2,at,:]=s
            return jnp.maximum(peak,jnp.max(s.reshape(rows//8,8,queries),0))
        peak=lax.fori_loop(0,blocks,scores,jnp.full((8,queries),-jnp.inf,F32),unroll=4)
        peak=jnp.max(peak,0,keepdims=True)
        def probs(b,total):
            at=pl.ds(pl.multiple_of(b*rows,rows),rows)
            p=jnp.exp2(score_ref[h%2,at,:]-peak)
            prob_ref[h%2,at,:]=p.astype(BF16)
            return total+jnp.sum(p.reshape(rows//8,8,queries),0)
        total=lax.fori_loop(0,blocks,probs,jnp.zeros((8,queries),F32),unroll=4)
        total=jnp.sum(total,0,keepdims=True)
        out=dot_nn(values_t,prob_ref[h%2])*(1.0/total)
        out_ref[:,h*head:(h+1)*head]=out.T.astype(BF16)
        log_ref[0,h:h+1,:]=peak+jnp.log2(total)

def attend_forward(queries, keyval, limits, bases, rows):
    seqs,keys,two=keyval.shape
    head=two//2; heads=queries.shape[1]//head; count=queries.shape[0]//seqs
    return pl.pallas_call(
        functools.partial(attend_kernel,rows,heads,head),
        grid_spec=pltpu.PrefetchScalarGridSpec(
            num_scalar_prefetch=1, grid=(seqs,),
            in_specs=[pl.BlockSpec((1,1,count),lambda i,*_:(i,0,0)),
                      pl.BlockSpec((count,heads*head),lambda i,*_:(i,0)),
                      pl.BlockSpec((1,keys,two),lambda i,*_:(i,0,0))],
            out_specs=[pl.BlockSpec((count,heads*head),lambda i,*_:(i,0)),
                       pl.BlockSpec((1,heads,count),lambda i,*_:(i,0,0))],
            scratch_shapes=[pltpu.VMEM((2,keys,count),F32),pltpu.VMEM((2,keys,count),BF16)]),
        out_shape=[jax.ShapeDtypeStruct(queries.shape,BF16),jax.ShapeDtypeStruct((seqs,heads,count),F32)],
        compiler_params=pltpu.CompilerParams(vmem_limit_bytes=40*2**20),
        cost_estimate=pl.CostEstimate(flops=4*queries.shape[0]*heads*head*keys,bytes_accessed=4*queries.size+2*keyval.size,transcendentals=queries.shape[0]*heads*keys),
    )(bases,limits,queries,keyval)

def attend_grad_kernel(
    rows, heads, head, base_ref, limit_ref, query_ref, grad_ref, log_ref, keyval_ref,
    dq_ref, dkv_ref, prob_ref, score_ref, exact_ref, slope_ref,
):
    keys = keyval_ref.shape[1]
    queries = query_ref.shape[0]
    blocks = keys // rows
    scale = head**-0.5
    limit = limit_ref[0]
    offset = lax.broadcasted_iota(jnp.int32, (rows, queries), 0)
    keys_t = keyval_ref[0, :, :head].T
    for h in range(heads):
        cols = slice(h * head, (h + 1) * head)
        lanes = slice(h * queries, (h + 1) * queries)
        query = query_ref[:, cols]
        grad = grad_ref[:, cols]
        log = log_ref[0, h : h + 1, :]

        def first(b, weighted):
            at = pl.ds(pl.multiple_of(b * rows, rows), rows)
            s = dot_nt(keyval_ref[0, at, :head], query) * (scale * LOG2E) - log
            s = jnp.where(offset <= limit - base_ref[b], s, NEGATIVE)
            p = jnp.exp2(s)
            dp = dot_nt(keyval_ref[0, at, head:], grad)
            prob_ref[at, lanes] = p.astype(BF16)
            exact_ref[h % 2, at, :] = p
            slope_ref[h % 2, at, :] = dp
            return weighted + jnp.sum((p * dp).reshape(rows // 8, 8, queries), 0)

        weighted = jnp.zeros((8, queries), F32)
        weighted = lax.fori_loop(0, blocks, first, weighted, unroll=4)
        weighted = jnp.sum(weighted, 0, keepdims=True)

        def second(b, carry):
            at = pl.ds(pl.multiple_of(b * rows, rows), rows)
            term = exact_ref[h % 2, at, :] * ((slope_ref[h % 2, at, :] - weighted) * scale)
            score_ref[at, lanes] = term.astype(BF16)
            return carry

        lax.fori_loop(0, blocks, second, 0, unroll=4)
        dq_ref[:, cols] = dot_nn(keys_t, score_ref[:, lanes]).T.astype(BF16)
    stacked_q = jnp.concatenate(
        [query_ref[:, h * head : (h + 1) * head] for h in range(heads)], 0
    )
    stacked_g = jnp.concatenate([grad_ref[:, h * head : (h + 1) * head] for h in range(heads)], 0)
    dkv_ref[0, :, :head] = dot_nn(score_ref[...], stacked_q).astype(BF16)
    dkv_ref[0, :, head:] = dot_nn(prob_ref[...], stacked_g).astype(BF16)


def attend_backward(queries, grad, logs, keyval, limits, bases, rows):
    seqs,keys,two=keyval.shape
    head=two//2; heads=queries.shape[1]//head; count=queries.shape[0]//seqs
    q_spec=pl.BlockSpec((count,heads*head),lambda i,*_:(i,0))
    return pl.pallas_call(
        functools.partial(attend_grad_kernel,rows,heads,head),
        grid_spec=pltpu.PrefetchScalarGridSpec(
            num_scalar_prefetch=1, grid=(seqs,),
            in_specs=[pl.BlockSpec((1,1,count),lambda i,*_:(i,0,0)),q_spec,q_spec,
                      pl.BlockSpec((1,heads,count),lambda i,*_:(i,0,0)),
                      pl.BlockSpec((1,keys,two),lambda i,*_:(i,0,0))],
            out_specs=[q_spec,pl.BlockSpec((1,keys,two),lambda i,*_:(i,0,0))],
            scratch_shapes=[pltpu.VMEM((keys,heads*count),BF16),pltpu.VMEM((keys,heads*count),BF16),pltpu.VMEM((2,keys,count),F32),pltpu.VMEM((2,keys,count),F32)]),
        out_shape=[jax.ShapeDtypeStruct(queries.shape,BF16),jax.ShapeDtypeStruct(keyval.shape,BF16)],
        compiler_params=pltpu.CompilerParams(vmem_limit_bytes=40*2**20),
        cost_estimate=pl.CostEstimate(flops=10*queries.shape[0]*heads*head*keys,bytes_accessed=8*queries.size+4*keyval.size,transcendentals=queries.shape[0]*heads*keys),
    )(bases,limits,queries,grad,logs,keyval)


def gather_keyval(block):
    even, odd = gather_dp(block)
    mine = jnp.concatenate([even, odd], 0)
    parts = [mine] + [swap_quad(mine, k) for k in range(1, quad_size())]
    return jnp.stack(parts).reshape(lax.axis_size("section"), -1, block.shape[-1]), even


def scatter_keyval(partial, rows):
    count = lax.axis_size("dp")
    blocks = partial.reshape(quad_size(), count * rows, partial.shape[-1])
    total = blocks[0]
    for k in range(1, quad_size()):
        total = total + swap_quad(blocks[k].astype(BF16), k).astype(F32)
    halves = total.reshape(2, count // 2, rows, partial.shape[-1])
    return scatter_dp(halves[0], halves[1])


def send_chips(block, pairs):
    return lax.ppermute(block, "dp", [(2 * a + c, 2 * b + c) for a, b in pairs for c in (0, 1)])


def gather_chips(block):
    chips = lax.axis_size("dp") // 2
    if chips != 4:
        return [block] + [swap_dp(block, 2 * j) for j in range(1, chips)]
    two = send_chips(block, [(0, 2), (2, 0), (1, 3), (3, 1)])
    one = send_chips(block, [(0, 1), (1, 0), (2, 3), (3, 2)])
    three = send_chips(block, [(1, 2), (2, 1)])
    return [block, one, two, three + send_chips(two, [(2, 3), (1, 0)])]


def gather_cores(far):
    count = lax.axis_size("dp")
    place = lax.axis_index("dp")
    near = swap_dp(jnp.stack(far), 1)
    whole = jnp.zeros((count,) + far[0].shape, far[0].dtype)
    for j in range(count // 2):
        whole = lax.dynamic_update_slice_in_dim(whole, far[j][None], place ^ (2 * j), 0)
        whole = lax.dynamic_update_slice_in_dim(whole, near[j][None], place ^ (2 * j + 1), 0)
    return whole.reshape((-1,) + far[0].shape[1:])


def scatter_mat(partial):
    chips = lax.axis_size("dp") // 2
    place = lax.axis_index("dp")
    core, chip = place % 2, place // 2
    pairs = partial.reshape(chips, 2, -1, partial.shape[1])
    kept = lax.dynamic_index_in_dim(pairs, core, 1, keepdims=False).astype(F32)
    given = lax.dynamic_index_in_dim(pairs, 1 - core, 1, keepdims=False)
    kept = (kept + swap_dp(given, 1).astype(F32)).astype(BF16)

    def piece(j):
        return lax.dynamic_index_in_dim(kept, chip ^ j, 0, keepdims=False)

    total = piece(0).astype(F32)
    if chips != 4:
        for j in range(1, chips):
            total = total + swap_dp(piece(j), 2 * j).astype(F32)
        return total
    passed = send_chips(piece(3), [(0, 1), (3, 2)])
    one = send_chips(piece(1), [(0, 1), (1, 0), (2, 3), (3, 2)])
    three = send_chips(piece(3), [(1, 2), (2, 1)])
    two = (piece(2).astype(F32) + passed.astype(F32)).astype(BF16)
    two = send_chips(two, [(0, 2), (2, 0), (1, 3), (3, 1)])
    return total + one.astype(F32) + two.astype(F32) + three.astype(F32)


def after(value, *done):
    held = lax.optimization_barrier((value,) + done)
    return held[0], held[1:]


def attend_part(inputs, pair, keyval_mat, norms, limits, bases):
    rows = inputs.shape[0]
    normed = layer_norm(inputs, norms[0], norms[1]).astype(BF16)
    keyval, passed = gather_keyval(dot_nn(normed, keyval_mat).astype(BF16))
    normed_all = spread(normed)
    queries = dot_nn(normed_all, pair[0]).astype(BF16)
    attended, logs = attend_forward(queries, keyval, limits, bases, rows)
    middle = inputs + collect(dot_nt(attended, pair[1]).astype(BF16))
    return middle, (normed_all, keyval, queries, logs, attended), passed


def feed_forward(middle, hidden_mat, project_mat, norms, whole):
    mixed = spread_blocks(layer_norm(middle, norms[2], norms[3]).astype(BF16))
    if whole:
        mixed = [jnp.concatenate(mixed, 0)]
    pre = [dot_nn(block, hidden_mat) for block in mixed]
    act = [gelu_tanh(block).astype(BF16) for block in pre]
    products = [dot_nn(block, project_mat).astype(BF16) for block in act]
    if whole:
        products = jnp.split(products[0], quad_size(), 0)
    return middle + collect_blocks(products), (middle, mixed, pre, act)


def scatter_rows(partial):
    return lax.psum_scatter(partial, "dp", scatter_dimension=0, tiled=True)


def scatter_columns(partial):
    return lax.psum_scatter(partial, "dp", scatter_dimension=1, tiled=True)


def layer_backward(inputs, grad_out, weights, limits, bases, saved, early, late):
    pair, keyval_mat, hidden_mat, project_mat, norms = weights
    normed_all, keyval, queries, logs, attended, middle, mixed_all, hidden_pre, hidden_act = saved
    rows = inputs.shape[0]
    branch = spread_blocks(grad_out.astype(BF16))
    if len(hidden_pre) == 1:
        branch = [jnp.concatenate(branch, 0)]
    pre = [
        jax.vjp(gelu_tanh, values)[1](dot_nt(block, project_mat))[0].astype(BF16)
        for values, block in zip(hidden_pre, branch)
    ]
    grad_branch, grad_pre = jnp.concatenate(branch, 0), jnp.concatenate(pre, 0)
    if len(pre) == 1:
        pre = jnp.split(grad_pre, quad_size(), 0)
    grad_mixed = collect_blocks([dot_nt(block, hidden_mat) for block in pre])
    hidden_act, _ = after(jnp.concatenate(hidden_act, 0), *early)
    mixed_all, _ = after(jnp.concatenate(mixed_all, 0), *early)
    grad_project = dot_tn(hidden_act, grad_branch).astype(BF16)
    sum_project = scatter_columns(grad_project)
    grad_hidden = dot_tn(mixed_all, grad_pre).astype(BF16)
    sum_hidden = scatter_rows(grad_hidden)
    if not early:
        grad_mixed, _ = after(grad_mixed, grad_project)
    pull = jax.vjp(layer_norm, middle, norms[2], norms[3])[1]
    grad_mid, grad_gain_two, grad_bias_two = pull(grad_mixed)
    grad_middle = grad_out + grad_mid
    grad_rows = spread(grad_middle.astype(BF16))
    grad_attended = dot_nt(grad_rows, pair[1].T).astype(BF16)
    grad_output = dot_tn(grad_rows, attended).astype(BF16)
    held = (grad_output, grad_project, grad_hidden) + late
    grad_attended, (grad_output, *_) = after(grad_attended, *held)
    grad_queries, grad_kv = attend_backward(
        queries, grad_attended, logs, keyval, limits, bases, rows
    )
    grad_normed = collect(dot_nt(grad_queries, pair[0]).astype(BF16))
    grad_query = dot_tn(normed_all, grad_queries).astype(BF16)
    grad_normed, (grad_query,) = after(grad_normed, grad_query)
    grad_pair = jnp.concatenate([grad_query, grad_output], 1)
    grad_keyval = scatter_keyval(grad_kv, rows).astype(BF16)
    grad_pair, _ = after(grad_pair, grad_keyval)
    grad_normed = grad_normed + dot_nt(grad_keyval, keyval_mat)
    pull = jax.vjp(layer_norm, inputs, norms[0], norms[1])[1]
    grad_in, grad_gain_one, grad_bias_one = pull(grad_normed)
    table = jnp.stack([grad_gain_one, grad_bias_one, grad_gain_two, grad_bias_two])

    grad_small = dot_tn(normed_all, spread(grad_keyval)).astype(BF16)
    count, tensors = lax.axis_size("dp"), lax.axis_size("tensor")
    grad_small = grad_small.reshape(count, tensors, 2, -1, grad_small.shape[1])
    grad_small = lax.dynamic_index_in_dim(grad_small, lax.axis_index("tensor"), 1, keepdims=False)
    grad_small = lax.dynamic_index_in_dim(grad_small, lax.axis_index("section"), 1, keepdims=False)
    sum_small = scatter_mat(grad_small.reshape(-1, grad_small.shape[-1]))
    return grad_middle + grad_in, (sum_small, sum_hidden, sum_project), grad_pair, table


def local(ends_in, pieces, w_query, w_keyval, w_output, w_hidden, w_project, norm_params):
    section = lax.axis_index("section")
    tensor = lax.axis_index("tensor")
    place = lax.axis_index("dp")
    first = section == 0
    count, tensors = lax.axis_size("dp"), lax.axis_size("tensor")
    rows, width = ends_in.shape[2:]

    given = lax.dynamic_index_in_dim(ends_in[0], 1 - section, 0, keepdims=False)
    kept = lax.dynamic_index_in_dim(ends_in[0], section, 0, keepdims=False)
    taken = lax.ppermute(given, "section", [(0, 1), (1, 0)])
    inputs = jnp.where(first, kept, taken).astype(F32)
    cotangent = jnp.where(first, taken, kept).astype(F32)

    depth = w_keyval.shape[1]
    columns = w_keyval.shape[2]
    table = jnp.pad(norm_params[0].reshape(-1), (0, 16 * columns - 4 * depth))
    small, small_passed = gather_all(jnp.concatenate([w_keyval[0], table.reshape(16, columns)], 0))
    keyval_mats = small[..., :depth, :].reshape(2, width, columns)
    norms = small[..., depth:, :].reshape(2, count * tensors, 16 * columns)
    norms = norms[..., : 4 * depth].reshape(2, count * tensors, 4, depth)
    norms = jnp.swapaxes(norms, 1, 2).reshape(2, 4, width).astype(F32)

    def quarter(array, cut, index):
        size = array.shape[cut] // 2
        return lax.dynamic_slice_in_dim(array, index * size, size, cut)

    row = jnp.arange(rows, dtype=jnp.int32)
    turn = tensor ^ jnp.arange(tensors, dtype=jnp.int32)
    query_pos = ((place * tensors + turn)[:, None] * rows + row).reshape(-1)
    order = jnp.concatenate([jnp.arange(0, count, 2), jnp.arange(1, count, 2)]).astype(jnp.int32)
    bases = (((place ^ order)[None, :] * tensors + turn[:, None]) * rows).reshape(-1)
    limits = []
    for k in range(2):
        starts = lax.dynamic_index_in_dim(pieces, section ^ k, 0, keepdims=False)[:, None]
        inside = (query_pos >= starts) & (query_pos < starts + SPAN)
        limits.append(jnp.max(jnp.where(inside, starts + SPAN - 1, query_pos), 0))
    limits = jnp.stack(limits)[:, None]

    def both(pick):
        kept = pick(section)
        moved = lax.ppermute(pick(1 - section), "section", [(0, 1), (1, 0)])
        return jnp.where(first, kept, moved), jnp.where(first, moved, kept)

    output_turned = w_output[0].T
    query_both = both(
        lambda k: jnp.concatenate([quarter(w_query[0], 1, k), quarter(output_turned, 1, k)], 1)
    )
    hidden_shard, project_shard = w_hidden[0], w_project[0]
    hidden_both = both(lambda k: quarter(hidden_shard, 1, k))
    project_both = both(lambda k: quarter(project_shard, 0, k))
    def rows_of(array):
        return lax.all_gather(array, "dp", axis=0, tiled=True)

    def columns_of(array):
        return lax.all_gather(array, "dp", axis=1, tiled=True)

    pair_one = jnp.split(rows_of(query_both[0]), 2, axis=1)
    pair_two = jnp.split(rows_of(query_both[1]), 2, axis=1)
    hidden_both, _ = after(hidden_both, small_passed)

    middle_one, saved_one, passed = attend_part(
        inputs, pair_one, keyval_mats[0], norms[0], limits, bases
    )
    project_both, _ = after(project_both, passed)
    project_one = columns_of(project_both[0])
    hidden_two = rows_of(hidden_both[1])
    hidden_one = rows_of(hidden_both[0])
    between, fed_one = feed_forward(middle_one, hidden_one, project_one, norms[0], False)
    between = between.astype(BF16)
    project_two = columns_of(project_both[1])
    between = between.astype(F32)

    middle_two, saved_two, _ = attend_part(between, pair_two, keyval_mats[1], norms[1], limits, bases)
    cotangent, _ = after(cotangent, middle_two)
    outputs, fed_two = feed_forward(middle_two, hidden_two, project_two, norms[1], True)

    grad_between, sums_two, grad_pair, table_two = layer_backward(
        between,
        cotangent,
        (pair_two, keyval_mats[1], hidden_two, project_two, norms[1]),
        limits,
        bases,
        saved_two + fed_two,
        (),
        (),
    )
    grad_between = grad_between.astype(BF16)
    sum_pair_two = scatter_rows(grad_pair)
    grad_between = grad_between.astype(F32)
    grad_inputs, sums_one, grad_pair, table_one = layer_backward(
        inputs,
        grad_between,
        (pair_one, keyval_mats[0], hidden_one, project_one, norms[0]),
        limits,
        bases,
        saved_one + fed_one,
        sums_two[1:],
        (),
    )
    def move(value, layer):
        value = value.astype(BF16)
        return value, lax.ppermute(value, "section", [(1 - layer, layer)])

    small_two, hidden_moved_two, project_moved_two = (move(v, 1) for v in sums_two)
    pair_moved_two = move(sum_pair_two, 1)
    small_one, hidden_moved_one, project_moved_one = (move(v, 0) for v in sums_one)
    grad_pair, _ = after(
        grad_pair,
        grad_inputs,
        *hidden_moved_two,
        *project_moved_two,
        *hidden_moved_one,
        *project_moved_one
    )
    pair_moved_one = move(scatter_rows(grad_pair), 0)

    def merged(one, two, cut):
        pair = jnp.where(
            first, jnp.concatenate(one, cut), jnp.concatenate((two[1], two[0]), cut)
        )
        return pair.astype(F32)[None]

    def columns_half(moved, index):
        return tuple(jnp.split(value, 2, axis=1)[index] for value in moved)

    results = [
        merged(columns_half(pair_moved_one, 0), columns_half(pair_moved_two, 0), 1),
        merged(small_one, small_two, 0),
        merged(columns_half(pair_moved_one, 1), columns_half(pair_moved_two, 1), 1),
        merged(hidden_moved_one, hidden_moved_two, 1),
        merged(project_moved_one, project_moved_two, 0),
    ]

    tables = jnp.stack([table_one, table_two]).reshape(2, 4, count, tensors, depth)
    table_result = scatter_all(jnp.moveaxis(tables, 1, 3), F32)

    given = jnp.where(first, outputs, grad_inputs).astype(BF16)
    kept = jnp.where(first, grad_inputs, outputs)
    taken = lax.ppermute(given, "section", [(0, 1), (1, 0)]).astype(F32)
    ends_out = jnp.where(first, jnp.stack([kept, taken]), jnp.stack([taken, kept]))
    return (
        ends_out[None],
        results[0],
        results[1],
        jnp.swapaxes(results[2], 1, 2),
        results[3],
        results[4],
        table_result[None, :3],
        table_result[None, 3],
    )


def solution(mesh):
    placed = (
        P("section", None, ("dp", "tensor"), None),
        P(),
        P("section", "dp", "tensor"),
        P("section", ("dp", "tensor"), None),
        P("section", "tensor", "dp"),
        P("section", "dp", "tensor"),
        P("section", "tensor", "dp"),
        P("section", None, ("dp", "tensor")),
    )
    return jax.shard_map(
        local,
        mesh=mesh,
        in_specs=placed,
        out_specs=(
            P("section", None, ("dp", "tensor"), None),
            P("section", "dp", "tensor"),
            P("section", ("dp", "tensor"), None),
            P("section", "tensor", "dp"),
            P("section", "dp", "tensor"),
            P("section", "tensor", "dp"),
            P("section", None, ("dp", "tensor")),
            P("section", ("dp", "tensor")),
        ),
        check_vma=False,
    )
```

```python
import functools
import math

import jax
import jax.numpy as jnp
from jax import lax
from jax.experimental import pallas as pl
from jax.experimental.pallas import tpu as pltpu
from jax.sharding import PartitionSpec as P

SPAN = 256
EPSILON = 1e-05
NEGATIVE = -1000000000.0
BF16 = jnp.bfloat16
F32 = jnp.float32
LOG2E = math.log2(math.e)


def dot(left, right, dims):
    return lax.dot_general(left, right, ((dims[0], dims[1]), ((), ())), preferred_element_type=F32)


def swap_quad(block, offset):
    size = lax.axis_size("section") * lax.axis_size("tensor")
    return lax.ppermute(block, ("section", "tensor"), [(i, i ^ offset) for i in range(size)])


def swap_dp(block, offset):
    return lax.ppermute(block, "dp", [(i, i ^ offset) for i in range(lax.axis_size("dp"))])


def quad_size():
    return lax.axis_size("section") * lax.axis_size("tensor")


def spread_blocks(block):
    return [block] + [swap_quad(block, k) for k in range(1, quad_size())]


def spread(block):
    return jnp.concatenate(spread_blocks(block), 0)


def collect_blocks(blocks):
    total = blocks[0].astype(F32)
    for k in range(1, quad_size()):
        total = total + swap_quad(blocks[k].astype(BF16), k).astype(F32)
    return total


def collect(partial):
    return collect_blocks(jnp.split(partial, quad_size(), 0))


def gather_dp(block):
    count = lax.axis_size("dp")
    far = [block] + [swap_dp(block, 2 * j) for j in range(1, count // 2)]
    near = swap_dp(jnp.stack(far), 1)
    return jnp.stack(far), near


def scatter_dp(near_even, near_odd):
    halves = near_even + swap_dp(near_odd.astype(BF16), 1).astype(F32)
    total = halves[0]
    for j in range(1, halves.shape[0]):
        total = total + swap_dp(halves[j].astype(BF16), 2 * j).astype(F32)
    return total


def scatter_all(blocks, wire):
    sections, count, tensors = blocks.shape[:3]
    me_s, me_d, me_t = lax.axis_index("section"), lax.axis_index("dp"), lax.axis_index("tensor")

    def pick(s, t):
        one = lax.dynamic_index_in_dim(blocks, me_s ^ s, 0, keepdims=False)
        return lax.dynamic_index_in_dim(one, me_t ^ t, 1, keepdims=False)

    total = pick(0, 0)
    for k in range(1, sections * tensors):
        total = total + swap_quad(pick(k // tensors, k % tensors).astype(wire), k).astype(F32)
    pairs = total.reshape((count // 2, 2) + total.shape[1:])
    core = me_d % 2
    kept = lax.dynamic_index_in_dim(pairs, core, 1, keepdims=False)
    given = lax.dynamic_index_in_dim(pairs, 1 - core, 1, keepdims=False)
    kept = kept + swap_dp(given.astype(wire), 1).astype(F32)
    place = me_d // 2
    result = lax.dynamic_index_in_dim(kept, place, 0, keepdims=False)
    for j in range(1, count // 2):
        piece = lax.dynamic_index_in_dim(kept, place ^ j, 0, keepdims=False)
        result = result + swap_dp(piece.astype(wire), 2 * j).astype(F32)
    return result


def gather_all(block):
    count, tensors = lax.axis_size("dp"), lax.axis_size("tensor")
    me_s, me_d, me_t = lax.axis_index("section"), lax.axis_index("dp"), lax.axis_index("tensor")
    even, odd = gather_dp(block)
    mine = jnp.stack([even, odd], 1).reshape((count,) + block.shape)
    passed = even
    beside = swap_quad(mine, 1)
    across = swap_quad(mine, tensors)
    corner = swap_quad(across, 1)

    def ordered(bit, own, other):
        return jnp.where(bit == 0, jnp.stack([own, other]), jnp.stack([other, own]))

    parts = ordered(me_s, ordered(me_t, mine, beside), ordered(me_t, across, corner))
    whole = jnp.zeros_like(parts)
    for j in range(count):
        whole = lax.dynamic_update_slice_in_dim(whole, parts[:, :, j : j + 1], me_d ^ j, 2)
    return jnp.swapaxes(whole, 1, 2), passed


def layer_norm(values, scale_row, shift_row):
    centered = values - jnp.mean(values, -1, keepdims=True)
    spread_of = jnp.mean(centered * centered, -1, keepdims=True)
    return centered * lax.rsqrt(spread_of + EPSILON) * scale_row + shift_row


def gelu_tanh(values):
    return jax.nn.gelu(values, approximate=True)


def dot_nn(left, right):
    return dot(left, right, ((1,), (0,)))


def dot_nt(left, right):
    return dot(left, right, ((1,), (1,)))


def dot_tn(left, right):
    return dot(left, right, ((0,), (0,)))


def attend_kernel(rows, heads, head, base_ref, limit_ref, query_ref, keyval_ref, out_ref, log_ref, score_ref, prob_ref):
    keys=keyval_ref.shape[1]; queries=query_ref.shape[0]
    blocks=keys//rows
    scale=head**-0.5*LOG2E
    limit=limit_ref[0]
    offset=lax.broadcasted_iota(jnp.int32,(rows,queries),0)
    values_t=keyval_ref[0,:,head:].T
    for h in range(heads):
        query=query_ref[:,h*head:(h+1)*head]
        def scores(b,peak):
            at=pl.ds(pl.multiple_of(b*rows,rows),rows)
            s=dot_nt(keyval_ref[0,at,:head],query)*scale
            s=jnp.where(offset<=limit-base_ref[b],s,NEGATIVE)
            score_ref[h%2,at,:]=s
            return jnp.maximum(peak,jnp.max(s.reshape(rows//8,8,queries),0))
        peak=lax.fori_loop(0,blocks,scores,jnp.full((8,queries),-jnp.inf,F32),unroll=4)
        peak=jnp.max(peak,0,keepdims=True)
        def probs(b,total):
            at=pl.ds(pl.multiple_of(b*rows,rows),rows)
            p=jnp.exp2(score_ref[h%2,at,:]-peak)
            prob_ref[h%2,at,:]=p.astype(BF16)
            return total+jnp.sum(p.reshape(rows//8,8,queries),0)
        total=lax.fori_loop(0,blocks,probs,jnp.zeros((8,queries),F32),unroll=4)
        total=jnp.sum(total,0,keepdims=True)
        out=dot_nn(values_t,prob_ref[h%2])*(1.0/total)
        out_ref[:,h*head:(h+1)*head]=out.T.astype(BF16)
        log_ref[0,h:h+1,:]=peak+jnp.log2(total)

def attend_forward(queries, keyval, limits, bases, rows):
    seqs,keys,two=keyval.shape
    head=two//2; heads=queries.shape[1]//head; count=queries.shape[0]//seqs
    return pl.pallas_call(
        functools.partial(attend_kernel,rows,heads,head),
        grid_spec=pltpu.PrefetchScalarGridSpec(
            num_scalar_prefetch=1, grid=(seqs,),
            in_specs=[pl.BlockSpec((1,1,count),lambda i,*_:(i,0,0)),
                      pl.BlockSpec((count,heads*head),lambda i,*_:(i,0)),
                      pl.BlockSpec((1,keys,two),lambda i,*_:(i,0,0))],
            out_specs=[pl.BlockSpec((count,heads*head),lambda i,*_:(i,0)),
                       pl.BlockSpec((1,heads,count),lambda i,*_:(i,0,0))],
            scratch_shapes=[pltpu.VMEM((2,keys,count),F32),pltpu.VMEM((2,keys,count),BF16)]),
        out_shape=[jax.ShapeDtypeStruct(queries.shape,BF16),jax.ShapeDtypeStruct((seqs,heads,count),F32)],
        compiler_params=pltpu.CompilerParams(vmem_limit_bytes=40*2**20),
        cost_estimate=pl.CostEstimate(flops=4*queries.shape[0]*heads*head*keys,bytes_accessed=4*queries.size+2*keyval.size,transcendentals=queries.shape[0]*heads*keys),
    )(bases,limits,queries,keyval)

def attend_grad_kernel(
    rows, heads, head, base_ref, limit_ref, query_ref, grad_ref, log_ref, keyval_ref,
    dq_ref, dkv_ref, prob_ref, score_ref, exact_ref, slope_ref,
):
    keys = keyval_ref.shape[1]
    queries = query_ref.shape[0]
    blocks = keys // rows
    scale = head**-0.5
    limit = limit_ref[0]
    offset = lax.broadcasted_iota(jnp.int32, (rows, queries), 0)
    keys_t = keyval_ref[0, :, :head].T
    for h in range(heads):
        cols = slice(h * head, (h + 1) * head)
        lanes = slice(h * queries, (h + 1) * queries)
        query = query_ref[:, cols]
        grad = grad_ref[:, cols]
        log = log_ref[0, h : h + 1, :]

        def first(b, weighted):
            at = pl.ds(pl.multiple_of(b * rows, rows), rows)
            s = dot_nt(keyval_ref[0, at, :head], query) * (scale * LOG2E) - log
            s = jnp.where(offset <= limit - base_ref[b], s, NEGATIVE)
            p = jnp.exp2(s)
            dp = dot_nt(keyval_ref[0, at, head:], grad)
            prob_ref[at, lanes] = p.astype(BF16)
            exact_ref[h % 2, at, :] = p
            slope_ref[h % 2, at, :] = dp
            return weighted + jnp.sum((p * dp).reshape(rows // 8, 8, queries), 0)

        weighted = jnp.zeros((8, queries), F32)
        weighted = lax.fori_loop(0, blocks, first, weighted, unroll=4)
        weighted = jnp.sum(weighted, 0, keepdims=True)

        def second(b, carry):
            at = pl.ds(pl.multiple_of(b * rows, rows), rows)
            term = exact_ref[h % 2, at, :] * ((slope_ref[h % 2, at, :] - weighted) * scale)
            score_ref[at, lanes] = term.astype(BF16)
            return carry

        lax.fori_loop(0, blocks, second, 0, unroll=4)
        dq_ref[:, cols] = dot_nn(keys_t, score_ref[:, lanes]).T.astype(BF16)
    stacked_q = jnp.concatenate(
        [query_ref[:, h * head : (h + 1) * head] for h in range(heads)], 0
    )
    stacked_g = jnp.concatenate([grad_ref[:, h * head : (h + 1) * head] for h in range(heads)], 0)
    dkv_ref[0, :, :head] = dot_nn(score_ref[...], stacked_q).astype(BF16)
    dkv_ref[0, :, head:] = dot_nn(prob_ref[...], stacked_g).astype(BF16)


def attend_backward(queries, grad, logs, keyval, limits, bases, rows):
    seqs,keys,two=keyval.shape
    head=two//2; heads=queries.shape[1]//head; count=queries.shape[0]//seqs
    q_spec=pl.BlockSpec((count,heads*head),lambda i,*_:(i,0))
    return pl.pallas_call(
        functools.partial(attend_grad_kernel,rows,heads,head),
        grid_spec=pltpu.PrefetchScalarGridSpec(
            num_scalar_prefetch=1, grid=(seqs,),
            in_specs=[pl.BlockSpec((1,1,count),lambda i,*_:(i,0,0)),q_spec,q_spec,
                      pl.BlockSpec((1,heads,count),lambda i,*_:(i,0,0)),
                      pl.BlockSpec((1,keys,two),lambda i,*_:(i,0,0))],
            out_specs=[q_spec,pl.BlockSpec((1,keys,two),lambda i,*_:(i,0,0))],
            scratch_shapes=[pltpu.VMEM((keys,heads*count),BF16),pltpu.VMEM((keys,heads*count),BF16),pltpu.VMEM((2,keys,count),F32),pltpu.VMEM((2,keys,count),F32)]),
        out_shape=[jax.ShapeDtypeStruct(queries.shape,BF16),jax.ShapeDtypeStruct(keyval.shape,BF16)],
        compiler_params=pltpu.CompilerParams(vmem_limit_bytes=40*2**20),
        cost_estimate=pl.CostEstimate(flops=10*queries.shape[0]*heads*head*keys,bytes_accessed=8*queries.size+4*keyval.size,transcendentals=queries.shape[0]*heads*keys),
    )(bases,limits,queries,grad,logs,keyval)


def gather_keyval(block):
    even, odd = gather_dp(block)
    mine = jnp.concatenate([even, odd], 0)
    parts = [mine] + [swap_quad(mine, k) for k in range(1, quad_size())]
    return jnp.stack(parts).reshape(lax.axis_size("section"), -1, block.shape[-1]), even


def scatter_keyval(partial, rows):
    count = lax.axis_size("dp")
    blocks = partial.reshape(quad_size(), count * rows, partial.shape[-1])
    total = blocks[0]
    for k in range(1, quad_size()):
        total = total + swap_quad(blocks[k].astype(BF16), k).astype(F32)
    halves = total.reshape(2, count // 2, rows, partial.shape[-1])
    return scatter_dp(halves[0], halves[1])


def send_chips(block, pairs):
    return lax.ppermute(block, "dp", [(2 * a + c, 2 * b + c) for a, b in pairs for c in (0, 1)])


def gather_chips(block):
    chips = lax.axis_size("dp") // 2
    if chips != 4:
        return [block] + [swap_dp(block, 2 * j) for j in range(1, chips)]
    two = send_chips(block, [(0, 2), (2, 0), (1, 3), (3, 1)])
    one = send_chips(block, [(0, 1), (1, 0), (2, 3), (3, 2)])
    three = send_chips(block, [(1, 2), (2, 1)])
    return [block, one, two, three + send_chips(two, [(2, 3), (1, 0)])]


def gather_cores(far):
    count = lax.axis_size("dp")
    place = lax.axis_index("dp")
    near = swap_dp(jnp.stack(far), 1)
    whole = jnp.zeros((count,) + far[0].shape, far[0].dtype)
    for j in range(count // 2):
        whole = lax.dynamic_update_slice_in_dim(whole, far[j][None], place ^ (2 * j), 0)
        whole = lax.dynamic_update_slice_in_dim(whole, near[j][None], place ^ (2 * j + 1), 0)
    return whole.reshape((-1,) + far[0].shape[1:])


def scatter_mat(partial):
    chips = lax.axis_size("dp") // 2
    place = lax.axis_index("dp")
    core, chip = place % 2, place // 2
    pairs = partial.reshape(chips, 2, -1, partial.shape[1])
    kept = lax.dynamic_index_in_dim(pairs, core, 1, keepdims=False).astype(F32)
    given = lax.dynamic_index_in_dim(pairs, 1 - core, 1, keepdims=False)
    kept = (kept + swap_dp(given, 1).astype(F32)).astype(BF16)

    def piece(j):
        return lax.dynamic_index_in_dim(kept, chip ^ j, 0, keepdims=False)

    total = piece(0).astype(F32)
    if chips != 4:
        for j in range(1, chips):
            total = total + swap_dp(piece(j), 2 * j).astype(F32)
        return total
    passed = send_chips(piece(3), [(0, 1), (3, 2)])
    one = send_chips(piece(1), [(0, 1), (1, 0), (2, 3), (3, 2)])
    three = send_chips(piece(3), [(1, 2), (2, 1)])
    two = (piece(2).astype(F32) + passed.astype(F32)).astype(BF16)
    two = send_chips(two, [(0, 2), (2, 0), (1, 3), (3, 1)])
    return total + one.astype(F32) + two.astype(F32) + three.astype(F32)


def after(value, *done):
    held = lax.optimization_barrier((value,) + done)
    return held[0], held[1:]


def attend_part(inputs, pair, keyval_mat, norms, limits, bases):
    rows = inputs.shape[0]
    normed = layer_norm(inputs, norms[0], norms[1]).astype(BF16)
    keyval, passed = gather_keyval(dot_nn(normed, keyval_mat).astype(BF16))
    normed_all = spread(normed)
    queries = dot_nn(normed_all, pair[0]).astype(BF16)
    attended, logs = attend_forward(queries, keyval, limits, bases, rows)
    middle = inputs + collect(dot_nt(attended, pair[1]).astype(BF16))
    return middle, (normed_all, keyval, queries, logs, attended), passed


def feed_forward(middle, hidden_mat, project_mat, norms, whole):
    mixed = spread_blocks(layer_norm(middle, norms[2], norms[3]).astype(BF16))
    if whole:
        mixed = [jnp.concatenate(mixed, 0)]
    pre = [dot_nn(block, hidden_mat) for block in mixed]
    act = [gelu_tanh(block).astype(BF16) for block in pre]
    products = [dot_nn(block, project_mat).astype(BF16) for block in act]
    if whole:
        products = jnp.split(products[0], quad_size(), 0)
    return middle + collect_blocks(products), (middle, mixed, pre, act)


def core_sum(partial):
    count = lax.axis_size("dp")
    core = lax.axis_index("dp") % 2
    rows = partial.shape[0] // count

    def shards(index):
        return jnp.concatenate(
            [
                lax.dynamic_slice_in_dim(partial, (2 * j + index) * rows, rows, 0)
                for j in range(count // 2)
            ],
            0,
        )

    return (shards(core).astype(F32) + swap_dp(shards(1 - core), 1).astype(F32)).astype(BF16)


def scatter_line(partial):
    count = lax.axis_size("dp")
    lines = [[2 * i + core for i in range(count // 2)] for core in range(2)]
    return lax.psum_scatter(
        partial, "dp", scatter_dimension=0, axis_index_groups=lines, tiled=True
    )


def scatter_rows(partial):
    return lax.psum_scatter(partial, "dp", scatter_dimension=0, tiled=True)


def scatter_columns(partial):
    return lax.psum_scatter(partial, "dp", scatter_dimension=1, tiled=True)


def layer_backward(inputs, grad_out, weights, limits, bases, saved, early, late):
    pair, keyval_mat, hidden_mat, project_mat, norms = weights
    normed_all, keyval, queries, logs, attended, middle, mixed_all, hidden_pre, hidden_act = saved
    rows = inputs.shape[0]
    branch = spread_blocks(grad_out.astype(BF16))
    if len(hidden_pre) == 1:
        branch = [jnp.concatenate(branch, 0)]
    pre = [
        jax.vjp(gelu_tanh, values)[1](dot_nt(block, project_mat))[0].astype(BF16)
        for values, block in zip(hidden_pre, branch)
    ]
    grad_branch, grad_pre = jnp.concatenate(branch, 0), jnp.concatenate(pre, 0)
    if len(pre) == 1:
        pre = jnp.split(grad_pre, quad_size(), 0)
    grad_mixed = collect_blocks([dot_nt(block, hidden_mat) for block in pre])
    hidden_act, _ = after(jnp.concatenate(hidden_act, 0), *early)
    mixed_all, _ = after(jnp.concatenate(mixed_all, 0), *early)
    grad_project = dot_tn(hidden_act, grad_branch).astype(BF16)
    sum_project = scatter_columns(grad_project)
    grad_hidden = dot_tn(mixed_all, grad_pre).astype(BF16)
    sum_hidden = scatter_rows(grad_hidden)
    if not early:
        grad_mixed, _ = after(grad_mixed, grad_project)
    pull = jax.vjp(layer_norm, middle, norms[2], norms[3])[1]
    grad_mid, grad_gain_two, grad_bias_two = pull(grad_mixed)
    grad_middle = grad_out + grad_mid
    grad_rows = spread(grad_middle.astype(BF16))
    grad_attended = dot_nt(grad_rows, pair[1].T).astype(BF16)
    grad_output = dot_tn(grad_rows, attended).astype(BF16)
    held = (grad_output, grad_project, grad_hidden) + late
    grad_attended, (grad_output, *_) = after(grad_attended, *held)
    grad_queries, grad_kv = attend_backward(
        queries, grad_attended, logs, keyval, limits, bases, rows
    )
    grad_normed = collect(dot_nt(grad_queries, pair[0]).astype(BF16))
    grad_query = dot_tn(normed_all, grad_queries).astype(BF16)
    grad_normed, (grad_query,) = after(grad_normed, grad_query)
    grad_pair = core_sum(jnp.concatenate([grad_query, grad_output], 1))
    grad_keyval = scatter_keyval(grad_kv, rows).astype(BF16)
    grad_pair, _ = after(grad_pair, grad_keyval)
    grad_normed = grad_normed + dot_nt(grad_keyval, keyval_mat)
    pull = jax.vjp(layer_norm, inputs, norms[0], norms[1])[1]
    grad_in, grad_gain_one, grad_bias_one = pull(grad_normed)
    table = jnp.stack([grad_gain_one, grad_bias_one, grad_gain_two, grad_bias_two])

    grad_small = dot_tn(normed_all, spread(grad_keyval)).astype(BF16)
    count, tensors = lax.axis_size("dp"), lax.axis_size("tensor")
    grad_small = grad_small.reshape(count, tensors, 2, -1, grad_small.shape[1])
    grad_small = lax.dynamic_index_in_dim(grad_small, lax.axis_index("tensor"), 1, keepdims=False)
    grad_small = lax.dynamic_index_in_dim(grad_small, lax.axis_index("section"), 1, keepdims=False)
    sum_small = scatter_mat(grad_small.reshape(-1, grad_small.shape[-1]))
    return grad_middle + grad_in, (sum_small, sum_hidden, sum_project), grad_pair, table


def local(ends_in, pieces, w_query, w_keyval, w_output, w_hidden, w_project, norm_params):
    section = lax.axis_index("section")
    tensor = lax.axis_index("tensor")
    place = lax.axis_index("dp")
    first = section == 0
    count, tensors = lax.axis_size("dp"), lax.axis_size("tensor")
    rows, width = ends_in.shape[2:]

    given = lax.dynamic_index_in_dim(ends_in[0], 1 - section, 0, keepdims=False)
    kept = lax.dynamic_index_in_dim(ends_in[0], section, 0, keepdims=False)
    taken = lax.ppermute(given, "section", [(0, 1), (1, 0)])
    inputs = jnp.where(first, kept, taken).astype(F32)
    cotangent = jnp.where(first, taken, kept).astype(F32)

    depth = w_keyval.shape[1]
    columns = w_keyval.shape[2]
    table = jnp.pad(norm_params[0].reshape(-1), (0, 16 * columns - 4 * depth))
    small, small_passed = gather_all(jnp.concatenate([w_keyval[0], table.reshape(16, columns)], 0))
    keyval_mats = small[..., :depth, :].reshape(2, width, columns)
    norms = small[..., depth:, :].reshape(2, count * tensors, 16 * columns)
    norms = norms[..., : 4 * depth].reshape(2, count * tensors, 4, depth)
    norms = jnp.swapaxes(norms, 1, 2).reshape(2, 4, width).astype(F32)

    def quarter(array, cut, index):
        size = array.shape[cut] // 2
        return lax.dynamic_slice_in_dim(array, index * size, size, cut)

    row = jnp.arange(rows, dtype=jnp.int32)
    turn = tensor ^ jnp.arange(tensors, dtype=jnp.int32)
    query_pos = ((place * tensors + turn)[:, None] * rows + row).reshape(-1)
    order = jnp.concatenate([jnp.arange(0, count, 2), jnp.arange(1, count, 2)]).astype(jnp.int32)
    bases = (((place ^ order)[None, :] * tensors + turn[:, None]) * rows).reshape(-1)
    limits = []
    for k in range(2):
        starts = lax.dynamic_index_in_dim(pieces, section ^ k, 0, keepdims=False)[:, None]
        inside = (query_pos >= starts) & (query_pos < starts + SPAN)
        limits.append(jnp.max(jnp.where(inside, starts + SPAN - 1, query_pos), 0))
    limits = jnp.stack(limits)[:, None]

    def both(pick):
        kept = pick(section)
        moved = lax.ppermute(pick(1 - section), "section", [(0, 1), (1, 0)])
        return jnp.where(first, kept, moved), jnp.where(first, moved, kept)

    output_turned = w_output[0].T
    query_both = both(
        lambda k: jnp.concatenate([quarter(w_query[0], 1, k), quarter(output_turned, 1, k)], 1)
    )
    hidden_shard, project_shard = w_hidden[0], w_project[0]
    hidden_both = both(lambda k: quarter(hidden_shard, 1, k))
    project_both = both(lambda k: quarter(project_shard, 0, k))
    def rows_of(array):
        return lax.all_gather(array, "dp", axis=0, tiled=True)

    def columns_of(array):
        return lax.all_gather(array, "dp", axis=1, tiled=True)

    pair_one = jnp.split(rows_of(query_both[0]), 2, axis=1)
    pair_two = jnp.split(rows_of(query_both[1]), 2, axis=1)
    hidden_both, _ = after(hidden_both, small_passed)

    middle_one, saved_one, passed = attend_part(
        inputs, pair_one, keyval_mats[0], norms[0], limits, bases
    )
    project_both, _ = after(project_both, passed)
    project_one = columns_of(project_both[0])
    hidden_two = rows_of(hidden_both[1])
    hidden_one = rows_of(hidden_both[0])
    between, fed_one = feed_forward(middle_one, hidden_one, project_one, norms[0], False)
    between = between.astype(BF16)
    project_two = columns_of(project_both[1])
    between = between.astype(F32)

    middle_two, saved_two, _ = attend_part(between, pair_two, keyval_mats[1], norms[1], limits, bases)
    cotangent, _ = after(cotangent, middle_two)
    outputs, fed_two = feed_forward(middle_two, hidden_two, project_two, norms[1], True)

    grad_between, sums_two, grad_pair, table_two = layer_backward(
        between,
        cotangent,
        (pair_two, keyval_mats[1], hidden_two, project_two, norms[1]),
        limits,
        bases,
        saved_two + fed_two,
        (),
        (),
    )
    grad_between = grad_between.astype(BF16)
    sum_pair_two = scatter_line(grad_pair)
    grad_between = grad_between.astype(F32)
    grad_inputs, sums_one, grad_pair, table_one = layer_backward(
        inputs,
        grad_between,
        (pair_one, keyval_mats[0], hidden_one, project_one, norms[0]),
        limits,
        bases,
        saved_one + fed_one,
        sums_two[1:],
        (),
    )
    def move(value, layer):
        value = value.astype(BF16)
        return value, lax.ppermute(value, "section", [(1 - layer, layer)])

    small_two, hidden_moved_two, project_moved_two = (move(v, 1) for v in sums_two)
    pair_moved_two = move(sum_pair_two, 1)
    small_one, hidden_moved_one, project_moved_one = (move(v, 0) for v in sums_one)
    grad_pair, _ = after(
        grad_pair,
        grad_inputs,
        *hidden_moved_two,
        *project_moved_two,
        *project_moved_one
    )
    pair_moved_one = move(scatter_line(grad_pair), 0)

    def merged(one, two, cut):
        pair = jnp.where(
            first, jnp.concatenate(one, cut), jnp.concatenate((two[1], two[0]), cut)
        )
        return pair.astype(F32)[None]

    def columns_half(moved, index):
        return tuple(jnp.split(value, 2, axis=1)[index] for value in moved)

    results = [
        merged(columns_half(pair_moved_one, 0), columns_half(pair_moved_two, 0), 1),
        merged(small_one, small_two, 0),
        merged(columns_half(pair_moved_one, 1), columns_half(pair_moved_two, 1), 1),
        merged(hidden_moved_one, hidden_moved_two, 1),
        merged(project_moved_one, project_moved_two, 0),
    ]

    tables = jnp.stack([table_one, table_two]).reshape(2, 4, count, tensors, depth)
    table_result = scatter_all(jnp.moveaxis(tables, 1, 3), F32)

    given = jnp.where(first, outputs, grad_inputs).astype(BF16)
    kept = jnp.where(first, grad_inputs, outputs)
    taken = lax.ppermute(given, "section", [(0, 1), (1, 0)]).astype(F32)
    ends_out = jnp.where(first, jnp.stack([kept, taken]), jnp.stack([taken, kept]))
    return (
        ends_out[None],
        results[0],
        results[1],
        jnp.swapaxes(results[2], 1, 2),
        results[3],
        results[4],
        table_result[None, :3],
        table_result[None, 3],
    )


def solution(mesh):
    placed = (
        P("section", None, ("dp", "tensor"), None),
        P(),
        P("section", "dp", "tensor"),
        P("section", ("dp", "tensor"), None),
        P("section", "tensor", "dp"),
        P("section", "dp", "tensor"),
        P("section", "tensor", "dp"),
        P("section", None, ("dp", "tensor")),
    )
    return jax.shard_map(
        local,
        mesh=mesh,
        in_specs=placed,
        out_specs=(
            P("section", None, ("dp", "tensor"), None),
            P("section", "dp", "tensor"),
            P("section", ("dp", "tensor"), None),
            P("section", "tensor", "dp"),
            P("section", "dp", "tensor"),
            P("section", "tensor", "dp"),
            P("section", None, ("dp", "tensor")),
            P("section", ("dp", "tensor")),
        ),
        check_vma=False,
    )
```
